256 devices in a mesh: energy: 64 (over x, z, core), chain: 4 (over y).
Axes of the slice: x: 4, y: 4, z: 8, core: 2. Of those that a mesh axis runs over, the one named last changes fastest.
Arguments:
- onsite: float32 [12, 256], P('chain'), may hold values from -4 to 4
- sigma_real: float32 [256, 12, 256], P('energy', 'chain'), may hold values from -2 to 2
- broadening: float32 [256, 12, 256], P('energy', 'chain'), may hold values from 1 to 2
- couplings: bfloat16 [12, 256, 256], P('chain'), may hold values from -0.5 to 0.5
- occupancy: float32 [256, 12], P('energy', 'chain'), may hold values from 0.05 to 0.95
- mode_weights: float32 [4, 128], replicated, may hold values from 0.2 to 1
- mode_shifts: int32 [4], replicated, may hold values from -24 to 24, as said below
Outputs:
- sigma_lesser: float32 [256, 12, 256, 128], P('energy', 'chain')
- sigma_greater: float32 [256, 12, 256, 128], P('energy', 'chain')
The draws below stay inside these ranges and needn't reach their ends.
Inputs may be any that keep to these rules, and one draw needn't show every extreme that they name: `mode_shifts`: the first mode shifts by exactly 24 points and the second by exactly -24.
All inputs are finite; a program needn't handle non-finite values.
Results may differ from the reference program's by a relative error of at most 0.0003.
Values sent between devices are 32-bit elements; how exact they have to be, the bound alone decides.
A program may use at most 128 MiB of HBM per device.

```python
import math
import jax
import jax.numpy as jnp
from jax import lax

ORB = 256
BAND = 128
MODES = 4
SHIFT_MAX = 24
SLABS = 12
ENERGIES = 256


def draw_mode_shifts(key, part):
    key = jax.random.fold_in(key, 7)
    others = jax.random.randint(key, (MODES,), -SHIFT_MAX, SHIFT_MAX + 1).astype(jnp.int32)
    ends = jnp.array([SHIFT_MAX, -SHIFT_MAX], jnp.int32)
    return jnp.concatenate([ends, others[2:]])


def block_levels(stream_key, dims, pieces, smallest, high):
    level = 1.0
    for dim, shards_of in pieces:
        draws = jax.random.uniform(jax.random.fold_in(jax.random.fold_in(stream_key, 6), dim), (shards_of,), jnp.float32, smallest / len(pieces), high / len(pieces))
        level = level * jnp.repeat(jnp.exp(draws), dims[dim] // shards_of).reshape((-1,) + (1,) * (len(dims) - 1 - dim))
    return level


def noise(rng, dims, spread, limit, shards=(), held_as=jnp.bfloat16):
    entries = spread * jax.random.normal(rng, dims, jnp.float32)
    if shards:
        entries = entries * block_levels(rng, dims, shards, -0.22, 0.18)
    return jnp.clip(entries, -limit, limit).astype(held_as)


def setup_inputs(seed: int = 0) -> dict:
    splits = jax.random.split(jax.random.key(seed), 8)
    onsite = noise(splits[0], (SLABS, ORB), 1.0, 4.0, ((0, 4),), jnp.float32)
    sigma_real = noise(splits[1], (ENERGIES, SLABS, ORB), 0.3, 2.0, ((0, 64), (1, 4)), jnp.float32)
    broadening = jnp.clip(jnp.exp(math.log(2.0) - 0.6931472 * jax.random.uniform(splits[2], (ENERGIES, SLABS, ORB), jnp.float32) ** block_levels(splits[2], (ENERGIES, SLABS, ORB), ((0, 64), (1, 4)), -0.2, 0.2)), 1.0, 2.0)
    couplings = noise(splits[3], (SLABS, ORB, ORB), (5 * ORB // 8) ** -0.5, 0.5, ((0, 4),))
    occupancy = jnp.clip(0.05 + 0.9 * jax.random.uniform(splits[4], (ENERGIES, SLABS), jnp.float32) ** block_levels(splits[4], (ENERGIES, SLABS), ((0, 64), (1, 4)), -0.2, 0.2), 0.05, 0.95)
    mode_weights = jnp.clip(jnp.exp(jax.random.uniform(splits[5], (MODES, BAND), jnp.float32, math.log(0.2), math.log(1.0))), 0.2, 1.0)
    mode_shifts = draw_mode_shifts(jax.random.fold_in(splits[7], 71), 0)
    return dict(onsite=onsite, sigma_real=sigma_real, broadening=broadening, couplings=couplings, occupancy=occupancy, mode_weights=mode_weights, mode_shifts=mode_shifts)


def band_of(matrix, band_width):
    leading = matrix.shape[0]
    orbitals = matrix.shape[1]
    widened = jnp.concatenate([matrix, matrix[:, :, :band_width]], axis=2).reshape(leading, -1)
    flattened = jnp.concatenate([widened, jnp.zeros((leading, orbitals), matrix.dtype)], axis=1)
    return flattened.reshape(leading, orbitals, orbitals + band_width + 1)[:, :, :band_width]


def sandwich(state, coupling):
    inner = jnp.einsum("eik,kl->eil", state, coupling, precision=lax.Precision.HIGHEST)
    return jnp.einsum("ij,eil->ejl", coupling, inner, precision=lax.Precision.HIGHEST)


def slab_step(state_real, state_imag, prop_real, prop_imag, coupling):
    mix_real = sandwich(state_real, coupling)
    mix_imag = sandwich(state_imag, coupling)
    outer_real = prop_real[:, :, None] * prop_real[:, None, :] - prop_imag[:, :, None] * prop_imag[:, None, :]
    outer_imag = prop_real[:, :, None] * prop_imag[:, None, :] + prop_imag[:, :, None] * prop_real[:, None, :]
    identity = jnp.eye(prop_real.shape[-1], dtype=jnp.float32)
    new_real = outer_real * mix_real - outer_imag * mix_imag + prop_real[:, :, None] * identity
    new_imag = outer_real * mix_imag + outer_imag * mix_real + prop_imag[:, :, None] * identity
    return new_real, new_imag


def reference(onsite, sigma_real, broadening, couplings, occupancy, mode_weights, mode_shifts):
    energies = -3.0 + 6.0 * (jnp.arange(ENERGIES).astype(jnp.float32) + 0.5) / ENERGIES
    detuning = energies[:, None, None] - onsite[None] - sigma_real
    denominator = detuning * detuning + broadening * broadening
    prop_real = detuning / denominator
    prop_imag = -broadening / denominator
    coupling_all = couplings.astype(jnp.float32)

    def advance(carry, inputs):
        state_real, state_imag = carry
        slab_real, slab_imag, coupling = inputs
        new_real, new_imag = slab_step(state_real, state_imag, slab_real, slab_imag, coupling)
        return (new_real, new_imag), -2.0 * band_of(new_imag, BAND)

    zeros = jnp.zeros((ENERGIES, ORB, ORB), jnp.float32)
    inputs = (jnp.swapaxes(prop_real, 0, 1), jnp.swapaxes(prop_imag, 0, 1), coupling_all)
    final_state, spectral = lax.scan(advance, (zeros, zeros), inputs)
    spectral = jnp.swapaxes(spectral, 0, 1)
    lesser = occupancy[:, :, None, None] * spectral
    greater = (1.0 - occupancy[:, :, None, None]) * spectral
    padding = ((SHIFT_MAX, SHIFT_MAX), (0, 0), (0, 0), (0, 0))
    lesser_padded = jnp.pad(lesser, padding)
    greater_padded = jnp.pad(greater, padding)
    sigma_lesser = jnp.zeros_like(lesser)
    sigma_greater = jnp.zeros_like(greater)
    for mode_index in range(MODES):
        weight_row = mode_weights[mode_index][None, None, None, :]
        shift_value = mode_shifts[mode_index].astype(jnp.int32)
        ahead = lax.dynamic_slice_in_dim(lesser_padded, (SHIFT_MAX + shift_value).astype(jnp.int32), ENERGIES, 0)
        behind = lax.dynamic_slice_in_dim(greater_padded, (SHIFT_MAX - shift_value).astype(jnp.int32), ENERGIES, 0)
        sigma_lesser = sigma_lesser + weight_row * ahead
        sigma_greater = sigma_greater + weight_row * behind
    return sigma_lesser, sigma_greater
```

```python
import functools

import jax
import jax.numpy as jnp
from jax import lax
from jax.experimental import pallas as pl
from jax.experimental.pallas import tpu as pltpu
from jax.sharding import PartitionSpec as P

ORB = 256
BAND = 128
SHIFT = 24
SLABS = 12
PLANES = 4
PER = 3
NSPEC = 6
LSET = (0, 1, 2, 3)
GSET = (0, 1, 4, 5)
BF = jnp.bfloat16
F32 = jnp.float32
MESH = pl.DeviceIdType.MESH


def split(value):
    high = value.astype(BF)
    low = (value - high.astype(F32)).astype(BF)
    return high, low


def sweep_kernel(
    pr, pi, prv, piv, coup, wl, wg, out_l, out_g,
    state, wide, band, stage, send_sem, recv_sem,
):
    me_e = lax.axis_index("energy")
    me_y = lax.axis_index("chain")
    rows = lax.broadcasted_iota(jnp.int32, (ORB, ORB), 0)
    cols = lax.broadcasted_iota(jnp.int32, (ORB, ORB), 1)
    anti = rows + cols == ORB - 1
    flip = jnp.where(anti, 1.0, 0.0).astype(BF)
    flip8 = 7 - lax.broadcasted_iota(jnp.int32, (8, BAND), 0)
    outs = (out_l, out_g)

    barrier = pltpu.get_barrier_semaphore()
    for step in range(1, PLANES):
        pl.semaphore_signal(
            barrier, inc=1, device_id=(me_e, lax.rem(me_y + step, PLANES)), device_id_type=MESH
        )
    pl.semaphore_wait(barrier, PLANES - 1)

    def keep(k, gr, gi):
        high, low = split(gr)
        state[k, 0:ORB, 0:ORB] = high
        state[k, 0:ORB, ORB:] = low
        high, low = split(gi)
        state[k, ORB:, 0:ORB] = high
        state[k, ORB:, ORB:] = low
        band[k] = pltpu.roll(gi, 1, 1, stride=1, stride_axis=0)[:, :BAND]

    def remote(s, m):
        return pltpu.make_async_remote_copy(
            src_ref=stage.at[s, m],
            dst_ref=outs[m].at[me_y, lax.rem(s, PER)],
            send_sem=send_sem.at[s, m],
            recv_sem=recv_sem.at[me_y, lax.rem(s, PER), m],
            device_id=(me_e, s // PER),
            device_id_type=MESH,
        )

    def local(s, m):
        return pltpu.make_async_copy(
            stage.at[s, m], outs[m].at[me_y, lax.rem(s, PER)], send_sem.at[s, m]
        )

    def finish(s):
        for m, (w, ks) in enumerate(((wl, LSET), (wg, GSET))):
            for t in range(ORB // 8):
                x = sum(band[k, 8 * t : 8 * t + 8] * w[s, k : k + 1] for k in ks)
                x = jnp.take_along_axis(x, flip8, axis=0)
                u = ORB // 8 - 1 - t
                stage[s, m, 8 * u : 8 * u + 8] = x

        @pl.when(s // PER != me_y)
        def _():
            for m in range(2):
                remote(s, m).start()

        @pl.when(s // PER == me_y)
        def _():
            for m in range(2):
                local(s, m).start()

    for k in range(NSPEC):
        keep(
            k,
            jnp.where(anti, pr[0, k : k + 1], 0.0),
            jnp.where(anti, pi[0, k : k + 1], 0.0),
        )
    finish(0)

    def slab(s, _):
        columns = jnp.concatenate([prv[s], piv[s]], axis=0).T
        c = coup[s].astype(BF)
        ct = lax.dot_general(flip, c, (((1,), (1,)), ((), ())), preferred_element_type=F32)
        ct = jnp.dot(ct.astype(BF), flip, preferred_element_type=F32).astype(BF)
        c2 = jnp.concatenate([c, c], axis=0)
        ct2 = jnp.concatenate([ct, ct], axis=1)

        def first(k):
            inner = jnp.dot(state[k], c2, preferred_element_type=F32)
            high, low = split(inner)
            wide[k, 0, 0:ORB] = high[:ORB]
            wide[k, 0, ORB:] = low[:ORB]
            wide[k, 1, 0:ORB] = high[ORB:]
            wide[k, 1, ORB:] = low[ORB:]

        def second(k):
            hr = jnp.dot(ct2, wide[k, 0], preferred_element_type=F32)
            hi = jnp.dot(ct2, wide[k, 1], preferred_element_type=F32)
            rr = pr[s, k : k + 1]
            ri = pi[s, k : k + 1]
            cr = columns[:, k : k + 1]
            ci = columns[:, 8 + k : 9 + k]
            qr = hr * rr - hi * ri
            qi = hr * ri + hi * rr
            qr = jnp.where(anti, qr + 1.0, qr)
            keep(k, qr * cr - qi * ci, qr * ci + qi * cr)

        first(0)
        for k in range(NSPEC):
            if k + 1 < NSPEC:
                first(k + 1)
            second(k)
        finish(s)
        return 0

    lax.fori_loop(1, SLABS, slab, 0)

    def drain_sent(s, _):
        @pl.when(s // PER != me_y)
        def _():
            for m in range(2):
                remote(s, m).wait_send()

        @pl.when(s // PER == me_y)
        def _():
            for m in range(2):
                local(s, m).wait()

        return 0

    lax.fori_loop(0, SLABS, drain_sent, 0)

    def drain_got(i, _):
        source = lax.rem(me_y + 1 + i // PER, PLANES)
        at = lax.rem(i, PER)
        for m in range(2):
            pltpu.make_async_remote_copy(
                src_ref=stage.at[0, m],
                dst_ref=outs[m].at[source, at],
                send_sem=send_sem.at[0, m],
                recv_sem=recv_sem.at[source, at, m],
                device_id=(me_e, source),
                device_id_type=MESH,
            ).wait_recv()
        return 0

    lax.fori_loop(0, (PLANES - 1) * PER, drain_got, 0)


def sweep(pr, pi, prv, piv, coup, wl, wg):
    shape = jax.ShapeDtypeStruct((PLANES, PER, ORB, BAND), F32)
    vmem = pl.BlockSpec(memory_space=pltpu.VMEM)
    return pl.pallas_call(
        sweep_kernel,
        out_shape=(shape, shape),
        in_specs=[vmem] * 7,
        out_specs=(vmem, vmem),
        scratch_shapes=[
            pltpu.VMEM((NSPEC, 2 * ORB, 2 * ORB), BF),
            pltpu.VMEM((NSPEC, 2, 2 * ORB, ORB), BF),
            pltpu.VMEM((NSPEC, ORB, BAND), F32),
            pltpu.VMEM((SLABS, 2, ORB, BAND), F32),
            pltpu.SemaphoreType.DMA((SLABS, 2)),
            pltpu.SemaphoreType.DMA((PLANES, PER, 2)),
        ],
        compiler_params=pltpu.CompilerParams(
            collective_id=0, has_side_effects=True, vmem_limit_bytes=40 << 20
        ),
    )(pr, pi, prv, piv, coup, wl, wg)


def body(onsite, sigma_real, broadening, couplings, occupancy, mode_weights, mode_shifts):
    count = sigma_real.shape[0]
    total = count * lax.axis_size("energy")
    me_e = lax.axis_index("energy")
    me_y = lax.axis_index("chain")
    index = jnp.arange(count) + me_e * count
    energies = -3.0 + 6.0 * (index.astype(F32) + 0.5) / total
    detuning = energies[:, None, None] - onsite[None] - sigma_real
    denominator = detuning * detuning + broadening * broadening
    prop_real = detuning / denominator
    prop_imag = -broadening / denominator
    filled = jnp.broadcast_to(occupancy[:, :, None], (count, PER, BAND))
    packed = jnp.concatenate([prop_real, prop_imag, filled], axis=2)
    packed = lax.all_gather(packed, "energy", axis=0, tiled=True)
    s2, s3 = mode_shifts[2], mode_shifts[3]
    shifts = jnp.stack([jnp.int32(SHIFT), jnp.int32(-SHIFT), s2, s3, -s2, -s3])
    wanted = index[:, None] + shifts[None]
    picked = jnp.take(packed, jnp.clip(wanted, 0, total - 1), axis=0)
    picked = lax.all_to_all(picked, "chain", split_axis=0, concat_axis=2, tiled=True)[0]
    picked = jnp.swapaxes(picked, 0, 1)
    picked = jnp.pad(picked, ((0, 0), (0, 8 - NSPEC), (0, 0)))
    pr, pi = picked[:, :, :ORB], picked[:, :, ORB : 2 * ORB]
    fill = picked[:, :NSPEC, 2 * ORB :]
    mine = me_e * count + me_y + shifts
    inside = jnp.where((mine >= 0) & (mine < total), -2.0, 0.0)[None, :, None]
    w = mode_weights
    none = jnp.zeros_like(w[0])
    rows_l = jnp.stack([w[0], w[1], w[2], w[3], none, none])[None]
    rows_g = jnp.stack([w[1], w[0], none, none, w[2], w[3]])[None]
    pad = ((0, 0), (0, 8 - NSPEC), (0, 0))
    wl = jnp.pad(inside * fill * rows_l, pad)
    wg = jnp.pad(inside * (1.0 - fill) * rows_g, pad)
    coup = lax.all_gather(couplings.astype(F32), "chain", axis=0, tiled=True)
    return sweep(pr, pi, pr[:, :, ::-1], pi[:, :, ::-1], coup, wl, wg)


def solution(mesh):
    in_specs = (
        P("chain", None),
        P("energy", "chain", None),
        P("energy", "chain", None),
        P("chain", None, None),
        P("energy", "chain"),
        P(),
        P(),
    )
    out_specs = (P("energy", "chain", None, None), P("energy", "chain", None, None))
    return jax.shard_map(body, mesh=mesh, in_specs=in_specs, out_specs=out_specs, check_vma=False)
```

```python
import jax
import jax.numpy as jnp
from jax import lax
from jax.experimental import pallas as pl
from jax.experimental.pallas import tpu as pltpu
from jax.sharding import PartitionSpec as P

ORB = 256
HALF = 128
BAND = 128
SHIFT = 24
SLABS = 12
PLANES = 4
PER = 3
ENERGIES = 256
NEAR = 3
OWN = 3
PICK = 4
STEPS = 2 * SLABS
BF = jnp.bfloat16
F32 = jnp.float32
MESH = pl.DeviceIdType.MESH


def split(value):
    high = value.astype(BF)
    low = (value - high.astype(F32)).astype(BF)
    return high, low


def split3(value):
    high, rest = split(value)
    low = (value - high.astype(F32) - rest.astype(F32)).astype(BF)
    return high, rest, low


def dot(a, b):
    return jnp.dot(a, b, preferred_element_type=F32)


def dot_nt(a, b):
    return lax.dot_general(a, b, (((1,), (1,)), ((), ())), preferred_element_type=F32)


def sweep_kernel(
    shifts, filled, onsite, sigma_real, broadening, couplings, weights, out,
    win, picked, props, cfull, cmat, ctmat, state, wide, sent, got, band, stage,
    win_s, win_r, pick_s, pick_r, c1_s, c1_r, c2_s, c2_r, ex_s, ex_r, out_s, out_r,
):
    me_e = lax.axis_index("energy")
    me_y = lax.axis_index("chain")
    chips = lax.axis_size("energy") // 2
    chip = me_e // 2
    core = lax.rem(me_e, 2)
    sign = 1 - 2 * core
    other = me_e + sign

    rows = lax.broadcasted_iota(jnp.int32, (ORB, ORB), 0)
    cols = lax.broadcasted_iota(jnp.int32, (ORB, ORB), 1)
    anti = rows + cols == ORB - 1
    flip = jnp.where(anti, 1.0, 0.0).astype(BF)
    flip8 = 7 - lax.broadcasted_iota(jnp.int32, (8, BAND), 0)

    def near(j, k):
        return lax.rem(chip + j + chips, chips) * 2 + k

    def plane(step):
        return lax.rem(me_y + step, PLANES)

    barrier = pltpu.get_barrier_semaphore()
    count = 0
    for j in range(-NEAR, NEAR + 1):
        if j:
            for k in range(2):
                pl.semaphore_signal(barrier, inc=1, device_id=(near(j, k), me_y), device_id_type=MESH)
                count += 1
    for step in range(PLANES):
        for k in (me_e, other) if step else (other,):
            pl.semaphore_signal(barrier, inc=1, device_id=(k, plane(step)), device_id_type=MESH)
            count += 1

    mine = (2 * NEAR + core) * 4
    points = (me_e * 4 + lax.broadcasted_iota(jnp.int32, (4, ORB), 0)).astype(F32)
    energy = -3.0 + 6.0 * (points + 0.5) / ENERGIES
    for sl in range(PER):
        detuning = energy - onsite[sl : sl + 1] - sigma_real[sl]
        width = broadening[sl]
        scale = detuning * detuning + width * width
        real = detuning / scale
        imag = -width / scale
        for i in range(4):
            for h in range(2):
                lanes = slice(HALF * h, HALF * (h + 1))
                win[mine + i, 4 * sl + h : 4 * sl + h + 1] = real[i : i + 1, lanes]
                win[mine + i, 4 * sl + 2 + h : 4 * sl + 3 + h] = imag[i : i + 1, lanes]
            win[mine + i, 12 + sl : 13 + sl] = jnp.full((1, HALF), filled[i, sl], F32)
    for i in range(4):
        win[mine + i, 15:16] = jnp.zeros((1, HALF), F32)

    for j in range(PER):
        cfull[me_y * PER + j] = couplings[j].astype(F32)

    pl.semaphore_wait(barrier, count)

    def window(j, k):
        i = 2 * (j + NEAR) + k
        return pltpu.make_async_remote_copy(
            src_ref=win.at[pl.ds(mine, 4)],
            dst_ref=win.at[pl.ds(((NEAR - j) * 2 + core) * 4, 4)],
            send_sem=win_s.at[i],
            recv_sem=win_r.at[(NEAR - j) * 2 + core],
            device_id=(near(j, k), me_y),
            device_id_type=MESH,
        )

    def window_all(act):
        for j in (3, -3, 2, -2, 1, -1):
            for k in range(2):
                act(window(j, k))

        act(
            pltpu.make_async_remote_copy(
                src_ref=win.at[pl.ds(mine, 4)],
                dst_ref=win.at[pl.ds(mine, 4)],
                send_sem=win_s.at[2 * NEAR],
                recv_sem=win_r.at[2 * NEAR + core],
                device_id=(other, me_y),
                device_id_type=MESH,
            )
        )

    window_all(lambda c: c.start())

    def coupling_out(step, j):
        s = me_y * PER + j
        part = cfull.at[s, pl.ds(core * HALF, HALF)]
        return pltpu.make_async_remote_copy(
            src_ref=part,
            dst_ref=part,
            send_sem=c1_s.at[step - 1, j],
            recv_sem=c1_r.at[s],
            device_id=(me_e, plane(step)),
            device_id_type=MESH,
        )

    def coupling_sends(j, act):
        for step in (1, 3, 2):
            act(coupling_out(step, j))

    @pl.when(me_y > 0)
    def _():
        coupling_sends(0, lambda c: c.start())

    @pl.when(me_y == 0)
    def _():
        coupling_sends(1, lambda c: c.start())

    for i in range(2 * (2 * NEAR + 1)):
        arrival = pltpu.make_async_remote_copy(
            src_ref=win.at[pl.ds(mine, 4)],
            dst_ref=win.at[pl.ds(4 * i, 4)],
            send_sem=win_s.at[0],
            recv_sem=win_r.at[i],
            device_id=(other, me_y),
            device_id_type=MESH,
        )

        @pl.when(2 * NEAR + core != i)
        def _():
            arrival.wait_recv()

    s2 = shifts[2] * sign
    s3 = shifts[3] * sign
    offsets = (SHIFT * sign, s2, s3, -SHIFT * sign)
    for y in range(PLANES):
        for phase in range(2):
            for k in range(PICK):
                value = win[SHIFT + 4 * phase + y + offsets[k]]
                picked[y, :, phase * PICK + k, :] = value

    def pick_out(step):
        return pltpu.make_async_remote_copy(
            src_ref=picked.at[plane(step)],
            dst_ref=props.at[me_y],
            send_sem=pick_s.at[step],
            recv_sem=pick_r.at[me_y],
            device_id=(me_e, plane(step)),
            device_id_type=MESH,
        )

    pick_here = pltpu.make_async_copy(picked.at[me_y], props.at[me_y], pick_s.at[0])
    for step in (2, 1, 3):
        pick_out(step).start()
    pick_here.start()

    @pl.when(me_y > 0)
    def _():
        coupling_sends(1, lambda c: c.start())

    coupling_sends(2, lambda c: c.start())

    pick_here.wait()
    for step in range(1, PLANES):
        source = plane(step)
        pltpu.make_async_remote_copy(
            src_ref=picked.at[0],
            dst_ref=props.at[source],
            send_sem=pick_s.at[step],
            recv_sem=pick_r.at[source],
            device_id=(me_e, source),
            device_id_type=MESH,
        ).wait_recv()

    def pass_on(s):
        part = cfull.at[s, pl.ds(core * HALF, HALF)]
        return pltpu.make_async_remote_copy(
            src_ref=part,
            dst_ref=part,
            send_sem=c2_s.at[s],
            recv_sem=c2_r.at[s],
            device_id=(other, me_y),
            device_id_type=MESH,
        )

    def forward(s):
        @pl.when(s // PER != me_y)
        def _():
            part = cfull.at[s, pl.ds(core * HALF, HALF)]
            pltpu.make_async_remote_copy(
                src_ref=part,
                dst_ref=part,
                send_sem=c1_s.at[0, 0],
                recv_sem=c1_r.at[s],
                device_id=(me_e, s // PER),
                device_id_type=MESH,
            ).wait_recv()
            pass_on(s).start()

    def ready(s):
        @pl.when(s // PER != me_y)
        def _():
            part = cfull.at[s, pl.ds((1 - core) * HALF, HALF)]
            pltpu.make_async_remote_copy(
                src_ref=part,
                dst_ref=part,
                send_sem=c2_s.at[s],
                recv_sem=c2_r.at[s],
                device_id=(other, me_y),
                device_id_type=MESH,
            ).wait_recv()

    def keep(k, t, gr, gi):
        high, low = split(gr)
        state[k, 0:ORB, 0:ORB] = high
        state[k, 0:ORB, ORB:] = low
        high, low = split(gi)
        state[k, ORB:, 0:ORB] = high
        state[k, ORB:, ORB:] = low
        rolled = pltpu.roll(gi, 1, 1, stride=1, stride_axis=0)[:, :BAND]
        if k == 0:
            sent[t] = rolled
        else:
            band[lax.rem(t, 2), k - 1] = rolled

    def exchange(t):
        return pltpu.make_async_remote_copy(
            src_ref=sent.at[t],
            dst_ref=got.at[t],
            send_sem=ex_s.at[t],
            recv_sem=ex_r.at[t],
            device_id=(other, me_y),
            device_id_type=MESH,
        )

    def ship(t, owner):
        s = lax.rem(t, SLABS)
        return pltpu.make_async_remote_copy(
            src_ref=stage.at[t],
            dst_ref=out.at[core, me_y, lax.rem(s, PER)],
            send_sem=out_s.at[t],
            recv_sem=out_r.at[core, me_y, lax.rem(s, PER)],
            device_id=(owner, s // PER),
            device_id_type=MESH,
        )

    def ship_here(t):
        s = lax.rem(t, SLABS)
        return pltpu.make_async_copy(
            stage.at[t], out.at[core, me_y, lax.rem(s, PER)], out_s.at[t]
        )

    def shipping(t, phase, far, here):
        s = lax.rem(t, SLABS)
        owner = chip * 2 + phase
        stays = (s // PER == me_y) & (owner == me_e)

        @pl.when(stays)
        def _():
            here(ship_here(t))

        @pl.when(jnp.logical_not(stays))
        def _():
            far(ship(t, owner))

    def factors(phase):
        first = chip * 8 + 4 * phase + me_y
        result = []
        for k, m in enumerate((0, 2, 3, 1)):
            e = first + offsets[k]
            scale = jnp.where((e >= 0) & (e < ENERGIES), -2.0, 0.0)
            result.append(scale * weights[m : m + 1, :])
        return result

    core_f = core.astype(F32)
    sign_f = sign.astype(F32)

    def finish(t, phase):
        s = lax.rem(t, SLABS)
        exchange(t).wait_recv()
        fill = props[s // PER, 12 + lax.rem(s, PER)]
        w = []
        for k, factor in enumerate(factors(phase)):
            w.append(factor * (core_f + sign_f * fill[phase * PICK + k : phase * PICK + k + 1]))
        slot = lax.rem(t, 2)
        for i in range(ORB // 8):
            at = slice(8 * i, 8 * i + 8)
            x = sent[t, at] * w[0] + band[slot, 0, at] * w[1]
            x += band[slot, 1, at] * w[2] + got[t, at] * w[3]
            x = jnp.take_along_axis(x, flip8, axis=0)
            u = ORB // 8 - 1 - i
            stage[t, 8 * u : 8 * u + 8] = x
        shipping(t, phase, lambda c: c.start(), lambda c: c.start())

    def prop_rows(s, phase):
        p, sl = s // PER, lax.rem(s, PER)
        at = slice(phase * PICK, phase * PICK + OWN)
        tiles = [props[p, 4 * sl + q][at] for q in range(4)]
        return jnp.concatenate(tiles[:2], axis=1), jnp.concatenate(tiles[2:], axis=1)

    forward(1)
    forward(2)

    for phase in range(2):
        real, imag = prop_rows(0, phase)
        for k in range(OWN):
            keep(
                k,
                phase * SLABS,
                jnp.where(anti, real[k : k + 1], 0.0),
                jnp.where(anti, imag[k : k + 1], 0.0),
            )
        exchange(phase * SLABS).start()
        if phase:
            finish(phase * SLABS - 1, phase - 1)

        def slab(s, _, phase=phase):
            t = phase * SLABS + s
            if phase == 0:
                @pl.when(s < SLABS - 2)
                def _():
                    forward(s + 2)

                ready(s)
                c = cfull[s].astype(BF)
                ct = dot(dot_nt(flip, c).astype(BF), flip).astype(BF)
                cmat[s] = c
                ctmat[s] = ct
            c2 = jnp.concatenate([cmat[s], cmat[s]], axis=0)
            ct2 = jnp.concatenate([ctmat[s], ctmat[s]], axis=1)
            real, imag = prop_rows(s, phase)
            both = jnp.concatenate([real, imag, jnp.zeros((2, ORB), F32)], axis=0)
            columns = dot_nt(
                jnp.concatenate([flip, flip, flip], axis=1),
                jnp.concatenate(split3(both), axis=1),
            )

            def first(k):
                inner = dot(state[k], c2)
                high, low = split(inner)
                wide[k, 0, 0:ORB] = high[:ORB]
                wide[k, 0, ORB:] = low[:ORB]
                wide[k, 1, 0:ORB] = high[ORB:]
                wide[k, 1, ORB:] = low[ORB:]

            def second(k):
                hr = dot(ct2, wide[k, 0])
                hi = dot(ct2, wide[k, 1])
                rr = real[k : k + 1]
                ri = imag[k : k + 1]
                cr = columns[:, k : k + 1]
                ci = columns[:, OWN + k : OWN + k + 1]
                qr = hr * rr - hi * ri
                qi = hr * ri + hi * rr
                qr = jnp.where(anti, qr + 1.0, qr)
                keep(k, t, qr * cr - qi * ci, qr * ci + qi * cr)

            first(0)
            for k in range(OWN):
                if k + 1 < OWN:
                    first(k + 1)
                second(k)
            exchange(t).start()
            finish(t - 1, phase)
            return 0

        lax.fori_loop(1, SLABS, slab, 0)
    finish(STEPS - 1, 1)

    window_all(lambda c: c.wait_send())
    for step in range(1, PLANES):
        pick_out(step).wait_send()

    @pl.when(me_y > 0)
    def _():
        coupling_sends(0, lambda c: c.wait_send())

    coupling_sends(1, lambda c: c.wait_send())
    coupling_sends(2, lambda c: c.wait_send())

    def passed(s, _):
        @pl.when(s // PER != me_y)
        def _():
            pass_on(s).wait_send()

        return 0

    lax.fori_loop(1, SLABS, passed, 0)

    for phase in range(2):
        def shipped(s, _, phase=phase):
            t = phase * SLABS + s
            exchange(t).wait_send()
            shipping(t, phase, lambda c: c.wait_send(), lambda c: c.wait())
            return 0

        lax.fori_loop(0, SLABS, shipped, 0)

    def landed(i, _):
        k, y, sl = i // (PLANES * PER), lax.rem(i // PER, PLANES), lax.rem(i, PER)

        @pl.when((k != core) | (y != me_y))
        def _():
            pltpu.make_async_remote_copy(
                src_ref=stage.at[0],
                dst_ref=out.at[k, y, sl],
                send_sem=out_s.at[0],
                recv_sem=out_r.at[k, y, sl],
                device_id=(other, me_y),
                device_id_type=MESH,
            ).wait_recv()

        return 0

    lax.fori_loop(0, 2 * PLANES * PER, landed, 0)


def body(onsite, sigma_real, broadening, couplings, occupancy, mode_weights, mode_shifts):
    vmem = pl.BlockSpec(memory_space=pltpu.VMEM)
    smem = pl.BlockSpec(memory_space=pltpu.SMEM)
    dma = pltpu.SemaphoreType.DMA
    near = 2 * (2 * NEAR + 1)
    out = pl.pallas_call(
        sweep_kernel,
        out_shape=jax.ShapeDtypeStruct((2, PLANES, PER, ORB, BAND), F32),
        in_specs=[smem, smem] + [vmem] * 5,
        out_specs=pl.BlockSpec(memory_space=pl.ANY),
        scratch_shapes=[
            pltpu.VMEM((4 * near, 16, HALF), F32),
            pltpu.VMEM((PLANES, 16, 8, HALF), F32),
            pltpu.VMEM((PLANES, 16, 8, HALF), F32),
            pltpu.VMEM((SLABS, ORB, ORB), F32),
            pltpu.VMEM((SLABS, ORB, ORB), BF),
            pltpu.VMEM((SLABS, ORB, ORB), BF),
            pltpu.VMEM((OWN, 2 * ORB, 2 * ORB), BF),
            pltpu.VMEM((OWN, 2, 2 * ORB, ORB), BF),
            pltpu.VMEM((STEPS, ORB, BAND), F32),
            pltpu.VMEM((STEPS, ORB, BAND), F32),
            pltpu.VMEM((2, OWN - 1, ORB, BAND), F32),
            pltpu.VMEM((STEPS, ORB, BAND), F32),
            dma((near,)),
            dma((near,)),
            dma((PLANES,)),
            dma((PLANES,)),
            dma((PLANES - 1, PER)),
            dma((SLABS,)),
            dma((SLABS,)),
            dma((SLABS,)),
            dma((STEPS,)),
            dma((STEPS,)),
            dma((STEPS,)),
            dma((2, PLANES, PER)),
        ],
        compiler_params=pltpu.CompilerParams(
            collective_id=0, has_side_effects=True, vmem_limit_bytes=48 << 20
        ),
    )(mode_shifts, occupancy, onsite, jnp.swapaxes(sigma_real, 0, 1), jnp.swapaxes(broadening, 0, 1), couplings, mode_weights)
    return out[0], out[1]


def solution(mesh):
    in_specs = (
        P("chain", None),
        P("energy", "chain", None),
        P("energy", "chain", None),
        P("chain", None, None),
        P("energy", "chain"),
        P(),
        P(),
    )
    out_specs = (P("energy", "chain", None, None), P("energy", "chain", None, None))
    return jax.shard_map(body, mesh=mesh, in_specs=in_specs, out_specs=out_specs, check_vma=False)
```

```python
import jax
import jax.numpy as jnp
from jax import lax
from jax.experimental import pallas as pl
from jax.experimental.pallas import tpu as pltpu
from jax.sharding import PartitionSpec as P

ORB = 256
HALF = 128
BAND = 128
SHIFT = 24
SLABS = 12
PLANES = 4
PER = 3
ENERGIES = 256
NEAR = 3
OWN = 3
PICK = 4
STEPS = 2 * SLABS
ROW = 4
PIECE = HALF // ROW
BLOCKS = 2 * PLANES * PER
BF = jnp.bfloat16
F32 = jnp.float32
MESH = pl.DeviceIdType.MESH


def split(value):
    high = value.astype(BF)
    low = (value - high.astype(F32)).astype(BF)
    return high, low


def split3(value):
    high, rest = split(value)
    low = (value - high.astype(F32) - rest.astype(F32)).astype(BF)
    return high, rest, low


def dot(a, b):
    return jnp.dot(a, b, preferred_element_type=F32)


def dot_nt(a, b):
    return lax.dot_general(a, b, (((1,), (1,)), ((), ())), preferred_element_type=F32)


def sweep_kernel(
    shifts_in, filled_in, onsite_in, sigma_in, broadening_in, couplings_in, weights_in, out,
    shifts, filled, onsite, sigma_real, broadening, couplings, weights, cast,
    win, picked, props, cfull, cmat, ctmat, state, wide, sent, got, band, stage,
    in_s, win_s, win_r, join_s, join_r, pick_s, pick_r,
    c0_s, c1_s, c1_r, c2_s, c2_r, c3_s, c3_r, ex_s, ex_r, out_s, out_r,
):
    loads = [
        pltpu.make_async_copy(source, target, in_s.at[i])
        for i, (source, target) in enumerate(
            (
                (couplings_in, couplings),
                (onsite_in, onsite),
                (sigma_in, sigma_real),
                (broadening_in, broadening),
                (filled_in, filled),
                (weights_in, weights),
                (shifts_in, shifts),
            )
        )
    ]
    for load in loads:
        load.start()

    me_e = lax.axis_index("energy")
    me_y = lax.axis_index("chain")
    devices = lax.axis_size("energy")
    chips = devices // 2
    chip = me_e // 2
    core = lax.rem(me_e, 2)
    sign = 1 - 2 * core
    other = me_e + sign
    me_x = me_e // (devices // ROW)

    rows = lax.broadcasted_iota(jnp.int32, (ORB, ORB), 0)
    cols = lax.broadcasted_iota(jnp.int32, (ORB, ORB), 1)
    anti = rows + cols == ORB - 1
    flip = jnp.where(anti, 1.0, 0.0).astype(BF)
    flip8 = 7 - lax.broadcasted_iota(jnp.int32, (8, BAND), 0)

    def near(j):
        return lax.rem(chip + j + chips, chips) * 2 + core

    def beside(i):
        return lax.rem(me_e + i * (devices // ROW), devices)

    def plane(step):
        return lax.rem(me_y + step, PLANES)

    def remote(source, target, send_sem, recv_sem, e, y):
        return pltpu.make_async_remote_copy(
            src_ref=source,
            dst_ref=target,
            send_sem=send_sem,
            recv_sem=recv_sem,
            device_id=(e, y),
            device_id_type=MESH,
        )

    barrier = pltpu.get_barrier_semaphore()
    peers = [(near(j), me_y) for j in range(-NEAR, NEAR + 1) if j]
    peers += [(beside(i), me_y) for i in range(1, ROW)]
    peers += [(me_e, plane(step)) for step in range(1, PLANES)]
    peers += [(other, plane(step)) for step in range(PLANES)]
    for peer in peers:
        pl.semaphore_signal(barrier, inc=1, device_id=peer, device_id_type=MESH)

    mine = (2 * NEAR + core) * 4
    for load in loads[1:]:
        load.wait()
    points = (me_e * 4 + lax.broadcasted_iota(jnp.int32, (4, ORB), 0)).astype(F32)
    energy = -3.0 + 6.0 * (points + 0.5) / ENERGIES
    for sl in range(PER):
        detuning = energy - onsite[sl : sl + 1] - sigma_real[sl]
        width = broadening[sl]
        scale = detuning * detuning + width * width
        real = detuning / scale
        imag = -width / scale
        for i in range(4):
            for h in range(2):
                lanes = slice(HALF * h, HALF * (h + 1))
                win[mine + i, 4 * sl + h : 4 * sl + h + 1] = real[i : i + 1, lanes]
                win[mine + i, 4 * sl + 2 + h : 4 * sl + 3 + h] = imag[i : i + 1, lanes]
            win[mine + i, 12 + sl : 13 + sl] = jnp.broadcast_to(filled[i : i + 1, sl : sl + 1], (1, HALF))
    for i in range(4):
        win[mine + i, 15:16] = jnp.zeros((1, HALF), F32)

    loads[0].wait()
    for j in range(PER):
        cast[j] = couplings[j].astype(F32)

    pl.semaphore_wait(barrier, len(peers))

    def window(j):
        return remote(
            win.at[pl.ds(mine, 4)],
            win.at[pl.ds(((NEAR - j) * 2 + core) * 4, 4)],
            win_s.at[j + NEAR],
            win_r.at[NEAR - j],
            near(j),
            me_y,
        )

    def join(j):
        part = win.at[pl.ds(((NEAR + j) * 2 + core) * 4, 4)]
        return remote(part, part, join_s.at[j + NEAR], join_r.at[j + NEAR], other, me_y)

    def joined(j):
        part = win.at[pl.ds(((NEAR + j) * 2 + 1 - core) * 4, 4)]
        return remote(part, part, join_s.at[j + NEAR], join_r.at[j + NEAR], other, me_y)

    far_first = (3, -3, 2, -2, 1, -1)
    for j in far_first:
        window(j).start()
    join(0).start()

    piece = core * HALF + me_x * PIECE

    def part_of(s, x):
        return cfull.at[s, pl.ds(core * HALF + x * PIECE, PIECE)]

    def coupling_out(step, j):
        s = me_y * PER + j
        return remote(
            cast.at[j, pl.ds(piece, PIECE)],
            part_of(s, me_x),
            c1_s.at[step - 1, j],
            c1_r.at[s],
            me_e,
            plane(step),
        )

    def coupling_sends(j, act):
        for step in (1, 3, 2):
            act(coupling_out(step, j))

    @pl.when(me_y > 0)
    def _():
        coupling_sends(0, lambda c: c.start())

    coupling_sends(1, lambda c: c.start())
    coupling_sends(2, lambda c: c.start())

    def coupling_here(j, i):
        x = lax.rem(me_x + i, ROW)
        s = me_y * PER + j
        sem = c2_r.at[s, x] if i else c0_s.at[j]
        return pltpu.make_async_copy(
            cast.at[j, pl.ds(core * HALF + x * PIECE, PIECE)], part_of(s, x), sem
        )

    for j in range(PER):
        for i in range(ROW):
            coupling_here(j, i).start()

    def coupling_beside(s, i):
        part = part_of(s, me_x)
        return remote(part, part, c2_s.at[s, i - 1], c2_r.at[s, me_x], beside(i), me_y)

    for s in (1, 3, 6, 9, 2, 4, 7, 10, 5, 8, 11):
        @pl.when(s // PER != me_y)
        def _(s=s):
            part = part_of(s, me_x)
            remote(part, part, c1_s.at[0, 0], c1_r.at[s], me_e, s // PER).wait_recv()
            for i in (1, 3, 2):
                coupling_beside(s, i).start()

    for j in far_first[::-1]:
        part = win.at[pl.ds(((NEAR + j) * 2 + core) * 4, 4)]
        remote(part, part, win_s.at[0], win_r.at[NEAR + j], other, me_y).wait_recv()
        join(j).start()
    for j in (0,) + far_first[::-1]:
        joined(j).wait_recv()

    s2 = shifts[2] * sign
    s3 = shifts[3] * sign
    offsets = (SHIFT * sign, s2, s3, -SHIFT * sign)
    for y in range(PLANES):
        for phase in range(2):
            for k in range(PICK):
                value = win[SHIFT + 4 * phase + y + offsets[k]]
                picked[y, :, phase * PICK + k, :] = value

    def pick_out(step):
        return remote(
            picked.at[plane(step)],
            props.at[me_y],
            pick_s.at[step],
            pick_r.at[me_y],
            me_e,
            plane(step),
        )

    pick_here = pltpu.make_async_copy(picked.at[me_y], props.at[me_y], pick_s.at[0])
    for step in (2, 1, 3):
        pick_out(step).start()
    pick_here.start()

    def pass_on(s):
        part = cfull.at[s, pl.ds(core * HALF, HALF)]
        return remote(part, part, c3_s.at[s], c3_r.at[s], other, me_y)

    def forward(s):
        for i in range(1, ROW):
            x = lax.rem(me_x + i, ROW)
            part = part_of(s, x)
            remote(part, part, c1_s.at[0, 0], c2_r.at[s, x], other, me_y).wait_recv()
        pass_on(s).start()

    def ready(s):
        part = cfull.at[s, pl.ds((1 - core) * HALF, HALF)]
        remote(part, part, c3_s.at[s], c3_r.at[s], other, me_y).wait_recv()

    for j in range(PER):
        coupling_here(j, 0).wait()
    forward(1)
    forward(2)

    pick_here.wait()
    for step in range(1, PLANES):
        source = plane(step)
        remote(
            picked.at[0], props.at[source], pick_s.at[step], pick_r.at[source], me_e, source
        ).wait_recv()

    def keep(k, t, gr, gi):
        high, low = split(gr)
        state[k, 0:ORB, 0:ORB] = high
        state[k, 0:ORB, ORB:] = low
        high, low = split(gi)
        state[k, ORB:, 0:ORB] = high
        state[k, ORB:, ORB:] = low
        rolled = pltpu.roll(gi, 1, 1, stride=1, stride_axis=0)[:, :BAND]
        if k == 0:
            sent[t] = rolled
        else:
            band[t % 2, k - 1] = rolled

    def exchange(t):
        return remote(sent.at[t], got.at[t], ex_s.at[t], ex_r.at[t], other, me_y)

    def ship(t):
        phase, s = t // SLABS, t % SLABS
        p, sl = s // PER, s % PER
        here = 1 - (lax.rem(p - me_y + PLANES, PLANES) + PLANES - 1) // PLANES
        here = here * (core if phase else 1 - core)
        base = (core * PLANES + me_y) * PER + sl
        at = base + here * (BLOCKS + sl - base)
        owner = chip * 2 + phase
        return remote(
            stage.at[t], out.at[at], out_s.at[t], out_r.at[at], owner + here * sign, p
        )

    def ship_here(sl):
        at = (core * PLANES + me_y) * PER + sl
        return pltpu.make_async_copy(
            stage.at[core * SLABS + me_y * PER + sl], out.at[at], c0_s.at[sl]
        )

    def factors(phase):
        first = chip * 8 + 4 * phase + me_y
        result = []
        for k, m in enumerate((0, 2, 3, 1)):
            e = first + offsets[k]
            scale = jnp.where((e >= 0) & (e < ENERGIES), -2.0, 0.0)
            result.append(scale * weights[m : m + 1, :])
        return result

    core_f = core.astype(F32)
    sign_f = sign.astype(F32)

    def finish(t, phase):
        s = t % SLABS
        exchange(t).wait_recv()
        fill = props[s // PER, 12 + s % PER]
        w = []
        for k, factor in enumerate(factors(phase)):
            w.append(factor * (core_f + sign_f * fill[phase * PICK + k : phase * PICK + k + 1]))
        slot = t % 2
        for i in range(ORB // 8):
            at = slice(8 * i, 8 * i + 8)
            x = sent[t, at] * w[0] + band[slot, 0, at] * w[1]
            x += band[slot, 1, at] * w[2] + got[t, at] * w[3]
            x = jnp.take_along_axis(x, flip8, axis=0)
            u = ORB // 8 - 1 - i
            stage[t, 8 * u : 8 * u + 8] = x
        ship(t).start()

    def prop_rows(s, phase):
        p, sl = s // PER, s % PER
        at = slice(phase * PICK, phase * PICK + OWN)
        tiles = [props[p, 4 * sl + q][at] for q in range(4)]
        return jnp.concatenate(tiles[:2], axis=1), jnp.concatenate(tiles[2:], axis=1)

    for phase in range(2):
        real, imag = prop_rows(0, phase)
        for k in range(OWN):
            keep(
                k,
                phase * SLABS,
                jnp.where(anti, real[k : k + 1], 0.0),
                jnp.where(anti, imag[k : k + 1], 0.0),
            )
        exchange(phase * SLABS).start()
        if phase:
            finish(phase * SLABS - 1, phase - 1)

        def slab(s, phase=phase):
            t = phase * SLABS + s
            if phase == 0:
                if s + 2 < SLABS:
                    forward(s + 2)
                ready(s)
                c = cfull[s].astype(BF)
                ct = dot(dot_nt(flip, c).astype(BF), flip).astype(BF)
                cmat[s] = c
                ctmat[s] = ct
            c2 = jnp.concatenate([cmat[s], cmat[s]], axis=0)
            ct2 = jnp.concatenate([ctmat[s], ctmat[s]], axis=1)
            real, imag = prop_rows(s, phase)
            both = jnp.concatenate([real, imag, jnp.zeros((2, ORB), F32)], axis=0)
            columns = dot_nt(
                jnp.concatenate([flip, flip, flip], axis=1),
                jnp.concatenate(split3(both), axis=1),
            )

            def first(k):
                inner = dot(state[k], c2)
                high, low = split(inner)
                wide[k, 0, 0:ORB] = high[:ORB]
                wide[k, 0, ORB:] = low[:ORB]
                wide[k, 1, 0:ORB] = high[ORB:]
                wide[k, 1, ORB:] = low[ORB:]

            def second(k):
                hr = dot(ct2, wide[k, 0])
                hi = dot(ct2, wide[k, 1])
                rr = real[k : k + 1]
                ri = imag[k : k + 1]
                cr = columns[:, k : k + 1]
                ci = columns[:, OWN + k : OWN + k + 1]
                qr = hr * rr - hi * ri
                qi = hr * ri + hi * rr
                qr = jnp.where(anti, qr + 1.0, qr)
                keep(k, t, qr * cr - qi * ci, qr * ci + qi * cr)

            first(0)
            for k in range(OWN):
                if k + 1 < OWN:
                    first(k + 1)
                second(k)
            exchange(t).start()
            finish(t - 1, phase)

        for s in range(1, SLABS):
            slab(s)
    finish(STEPS - 1, 1)

    for sl in range(PER):
        ship_here(sl).start()

    for j in far_first:
        window(j).wait_send()
    for j in range(-NEAR, NEAR + 1):
        join(j).wait_send()
    for step in range(1, PLANES):
        pick_out(step).wait_send()

    @pl.when(me_y > 0)
    def _():
        coupling_sends(0, lambda c: c.wait_send())

    coupling_sends(1, lambda c: c.wait_send())
    coupling_sends(2, lambda c: c.wait_send())
    for i in range(1, ROW):
        @pl.when(me_y == 0)
        def _(i=i):
            coupling_here(0, i).wait()

    def passed(s, _):
        pass_on(s).wait_send()

        @pl.when(s // PER != me_y)
        def _():
            for i in range(1, ROW):
                coupling_beside(s, i).wait_send()

        return 0

    lax.fori_loop(1, SLABS, passed, 0)

    def shipped(t, _):
        exchange(t).wait_send()
        remote(stage.at[t], out.at[0], out_s.at[t], out_r.at[0], other, me_y).wait_send()
        return 0

    lax.fori_loop(0, STEPS, shipped, 0)

    def landed(i, _):
        @pl.when(i // PER != core * PLANES + me_y)
        def _():
            remote(stage.at[0], out.at[i], out_s.at[0], out_r.at[i], other, me_y).wait_recv()

        return 0

    lax.fori_loop(0, BLOCKS + PER, landed, 0)
    for sl in range(PER):
        ship_here(sl).wait()


def body(onsite, sigma_real, broadening, couplings, occupancy, mode_weights, mode_shifts):
    hbm = pl.BlockSpec(memory_space=pltpu.HBM)
    vmem = pltpu.VMEM
    dma = pltpu.SemaphoreType.DMA
    near = 2 * NEAR + 1
    out = pl.pallas_call(
        sweep_kernel,
        out_shape=jax.ShapeDtypeStruct((BLOCKS + PER, ORB, BAND), F32),
        in_specs=[hbm] * 7,
        out_specs=pl.BlockSpec(memory_space=pl.ANY),
        scratch_shapes=[
            pltpu.SMEM(mode_shifts.shape, jnp.int32),
            vmem(occupancy.shape, F32),
            vmem(onsite.shape, F32),
            vmem((PER, 4, ORB), F32),
            vmem((PER, 4, ORB), F32),
            vmem(couplings.shape, BF),
            vmem(mode_weights.shape, F32),
            vmem((PER, ORB, ORB), F32),
            vmem((8 * near, 16, HALF), F32),
            vmem((PLANES, 16, 8, HALF), F32),
            vmem((PLANES, 16, 8, HALF), F32),
            vmem((SLABS, ORB, ORB), F32),
            vmem((SLABS, ORB, ORB), BF),
            vmem((SLABS, ORB, ORB), BF),
            vmem((OWN, 2 * ORB, 2 * ORB), BF),
            vmem((OWN, 2, 2 * ORB, ORB), BF),
            vmem((STEPS, ORB, BAND), F32),
            vmem((STEPS, ORB, BAND), F32),
            vmem((2, OWN - 1, ORB, BAND), F32),
            vmem((STEPS, ORB, BAND), F32),
            dma((7,)),
            dma((near,)),
            dma((near,)),
            dma((near,)),
            dma((near,)),
            dma((PLANES,)),
            dma((PLANES,)),
            dma((PER,)),
            dma((PLANES - 1, PER)),
            dma((SLABS,)),
            dma((SLABS, ROW - 1)),
            dma((SLABS, ROW)),
            dma((SLABS,)),
            dma((SLABS,)),
            dma((STEPS,)),
            dma((STEPS,)),
            dma((STEPS,)),
            dma((BLOCKS + PER,)),
        ],
        compiler_params=pltpu.CompilerParams(
            collective_id=0, has_side_effects=True, vmem_limit_bytes=60 << 20
        ),
    )(
        mode_shifts,
        occupancy,
        onsite,
        jnp.swapaxes(sigma_real, 0, 1),
        jnp.swapaxes(broadening, 0, 1),
        couplings,
        mode_weights,
    )
    shape = (PLANES, PER, ORB, BAND)
    return out[:SLABS].reshape(shape), out[SLABS:BLOCKS].reshape(shape)


def solution(mesh):
    in_specs = (
        P("chain", None),
        P("energy", "chain", None),
        P("energy", "chain", None),
        P("chain", None, None),
        P("energy", "chain"),
        P(),
        P(),
    )
    out_specs = (P("energy", "chain", None, None), P("energy", "chain", None, None))
    return jax.shard_map(body, mesh=mesh, in_specs=in_specs, out_specs=out_specs, check_vma=False)
```

```python
import jax
import jax.numpy as jnp
from jax import lax
from jax.experimental import pallas as pl
from jax.experimental.pallas import tpu as pltpu
from jax.sharding import PartitionSpec as P

ORB = 256
HALF = 128
BAND = 128
SHIFT = 24
SLABS = 12
PLANES = 4
PER = 3
ENERGIES = 256
NEAR = 3
OWN = 3
PICK = 4
STEPS = 2 * SLABS
ROW = 4
PIECE = HALF // ROW
BLOCKS = 2 * PLANES * PER
BF = jnp.bfloat16
F32 = jnp.float32
MESH = pl.DeviceIdType.MESH


def split(value):
    high = value.astype(BF)
    low = (value - high.astype(F32)).astype(BF)
    return high, low


def split3(value):
    high, rest = split(value)
    low = (value - high.astype(F32) - rest.astype(F32)).astype(BF)
    return high, rest, low


def dot(a, b):
    return jnp.dot(a, b, preferred_element_type=F32)


def dot_nt(a, b):
    return lax.dot_general(a, b, (((1,), (1,)), ((), ())), preferred_element_type=F32)


def sweep_kernel(
    shifts_in, filled_in, onsite_in, sigma_in, broadening_in, couplings_in, weights_in, out,
    shifts, filled, onsite, sigma_real, broadening, couplings, weights, cast,
    win, picked, props, cfull, cmat, ctmat, state, wide, sent, got, band, stage,
    in_s, win_s, win_r, join_s, join_r, pick_s, pick_r,
    c0_s, c1_s, c1_r, c2_s, c2_r, c3_s, c3_r, ex_s, ex_r, out_s, out_r,
):
    loads = [
        pltpu.make_async_copy(source, target, in_s.at[i])
        for i, (source, target) in enumerate(
            (
                (couplings_in, couplings),
                (onsite_in, onsite),
                (sigma_in, sigma_real),
                (broadening_in, broadening),
                (filled_in, filled),
                (weights_in, weights),
                (shifts_in, shifts),
            )
        )
    ]
    for load in loads:
        load.start()

    me_e = lax.axis_index("energy")
    me_y = lax.axis_index("chain")
    devices = lax.axis_size("energy")
    chips = devices // 2
    chip = me_e // 2
    core = lax.rem(me_e, 2)
    sign = 1 - 2 * core
    other = me_e + sign
    me_x = me_e // (devices // ROW)

    rows = lax.broadcasted_iota(jnp.int32, (ORB, ORB), 0)
    cols = lax.broadcasted_iota(jnp.int32, (ORB, ORB), 1)
    anti = rows + cols == ORB - 1
    flip = jnp.where(anti, 1.0, 0.0).astype(BF)
    flip8 = 7 - lax.broadcasted_iota(jnp.int32, (8, BAND), 0)

    def near(j):
        return lax.rem(chip + j + chips, chips) * 2 + core

    def beside(i):
        return lax.rem(me_e + i * (devices // ROW), devices)

    def plane(step):
        return lax.rem(me_y + step, PLANES)

    def remote(source, target, send_sem, recv_sem, e, y):
        return pltpu.make_async_remote_copy(
            src_ref=source,
            dst_ref=target,
            send_sem=send_sem,
            recv_sem=recv_sem,
            device_id=(e, y),
            device_id_type=MESH,
        )

    barrier = pltpu.get_barrier_semaphore()
    peers = [(near(j), me_y) for j in range(-NEAR, NEAR + 1) if j]
    peers += [(beside(i), me_y) for i in range(1, ROW)]
    peers += [(me_e, plane(step)) for step in range(1, PLANES)]
    peers += [(other, plane(step)) for step in range(PLANES)]
    for peer in peers:
        pl.semaphore_signal(barrier, inc=1, device_id=peer, device_id_type=MESH)

    mine = (2 * NEAR + core) * 4
    for load in loads[1:]:
        load.wait()
    points = (me_e * 4 + lax.broadcasted_iota(jnp.int32, (4, ORB), 0)).astype(F32)
    energy = -3.0 + 6.0 * (points + 0.5) / ENERGIES
    for sl in range(PER):
        detuning = energy - onsite[sl : sl + 1] - sigma_real[sl]
        width = broadening[sl]
        scale = detuning * detuning + width * width
        real = detuning / scale
        imag = -width / scale
        for i in range(4):
            for h in range(2):
                lanes = slice(HALF * h, HALF * (h + 1))
                win[mine + i, 4 * sl + h : 4 * sl + h + 1] = real[i : i + 1, lanes]
                win[mine + i, 4 * sl + 2 + h : 4 * sl + 3 + h] = imag[i : i + 1, lanes]
            win[mine + i, 12 + sl : 13 + sl] = jnp.broadcast_to(filled[i : i + 1, sl : sl + 1], (1, HALF))
    for i in range(4):
        win[mine + i, 15:16] = jnp.zeros((1, HALF), F32)

    loads[0].wait()
    for j in range(PER):
        cast[j] = couplings[j].astype(F32)

    pl.semaphore_wait(barrier, len(peers))

    def window(j):
        return remote(
            win.at[pl.ds(mine, 4)],
            win.at[pl.ds(((NEAR - j) * 2 + core) * 4, 4)],
            win_s.at[j + NEAR],
            win_r.at[NEAR - j],
            near(j),
            me_y,
        )

    def join(j):
        part = win.at[pl.ds(((NEAR + j) * 2 + core) * 4, 4)]
        return remote(part, part, join_s.at[j + NEAR], join_r.at[j + NEAR], other, me_y)

    def joined(j):
        part = win.at[pl.ds(((NEAR + j) * 2 + 1 - core) * 4, 4)]
        return remote(part, part, join_s.at[j + NEAR], join_r.at[j + NEAR], other, me_y)

    far_first = (3, -3, 2, -2, 1, -1)
    for j in far_first:
        window(j).start()
    join(0).start()

    piece = core * HALF + me_x * PIECE

    def part_of(s, x):
        return cfull.at[s, pl.ds(core * HALF + x * PIECE, PIECE)]

    def coupling_out(step, j):
        s = me_y * PER + j
        return remote(
            cast.at[j, pl.ds(piece, PIECE)],
            part_of(s, me_x),
            c1_s.at[step - 1, j],
            c1_r.at[s],
            me_e,
            plane(step),
        )

    def coupling_sends(j, act):
        for step in (1, 3, 2):
            act(coupling_out(step, j))

    @pl.when(me_y > 0)
    def _():
        coupling_sends(0, lambda c: c.start())

    coupling_sends(1, lambda c: c.start())
    coupling_sends(2, lambda c: c.start())

    def coupling_here(j, i):
        x = lax.rem(me_x + i, ROW)
        s = me_y * PER + j
        sem = c2_r.at[s, x] if i else c0_s.at[j]
        return pltpu.make_async_copy(
            cast.at[j, pl.ds(core * HALF + x * PIECE, PIECE)], part_of(s, x), sem
        )

    for j in range(PER):
        for i in range(ROW):
            coupling_here(j, i).start()

    def coupling_beside(s, i):
        part = part_of(s, me_x)
        return remote(part, part, c2_s.at[s, i - 1], c2_r.at[s, me_x], beside(i), me_y)

    for s in (1, 3, 6, 9, 2, 4, 7, 10, 5, 8, 11):
        @pl.when(s // PER != me_y)
        def _(s=s):
            part = part_of(s, me_x)
            remote(part, part, c1_s.at[0, 0], c1_r.at[s], me_e, s // PER).wait_recv()
            for i in (1, 3, 2):
                coupling_beside(s, i).start()

    for j in far_first[::-1]:
        part = win.at[pl.ds(((NEAR + j) * 2 + core) * 4, 4)]
        remote(part, part, win_s.at[0], win_r.at[NEAR + j], other, me_y).wait_recv()
        join(j).start()
    for j in (0,) + far_first[::-1]:
        joined(j).wait_recv()

    s2 = shifts[2] * sign
    s3 = shifts[3] * sign
    offsets = (SHIFT * sign, s2, s3, -SHIFT * sign)
    for y in range(PLANES):
        for phase in range(2):
            for k in range(PICK):
                value = win[SHIFT + 4 * phase + y + offsets[k]]
                picked[y, :, phase * PICK + k, :] = value

    def pick_out(step):
        return remote(
            picked.at[plane(step)],
            props.at[me_y],
            pick_s.at[step],
            pick_r.at[me_y],
            me_e,
            plane(step),
        )

    pick_here = pltpu.make_async_copy(picked.at[me_y], props.at[me_y], pick_s.at[0])
    for step in (2, 1, 3):
        pick_out(step).start()
    pick_here.start()

    def pass_on(s):
        part = cfull.at[s, pl.ds(core * HALF, HALF)]
        return remote(part, part, c3_s.at[s], c3_r.at[s], other, me_y)

    def forward(s):
        for i in range(1, ROW):
            x = lax.rem(me_x + i, ROW)
            part = part_of(s, x)
            remote(part, part, c1_s.at[0, 0], c2_r.at[s, x], other, me_y).wait_recv()
        pass_on(s).start()

    def ready(s):
        part = cfull.at[s, pl.ds((1 - core) * HALF, HALF)]
        remote(part, part, c3_s.at[s], c3_r.at[s], other, me_y).wait_recv()

    for j in range(PER):
        coupling_here(j, 0).wait()
    forward(1)
    forward(2)

    pick_here.wait()
    for step in range(1, PLANES):
        source = plane(step)
        remote(
            picked.at[0], props.at[source], pick_s.at[step], pick_r.at[source], me_e, source
        ).wait_recv()

    def keep(k, t, gr, gi):
        high, low = split(gr)
        state[k, 0:ORB, 0:ORB] = high
        state[k, 0:ORB, ORB:] = low
        high, low = split(gi)
        state[k, ORB:, 0:ORB] = high
        state[k, ORB:, ORB:] = low
        rolled = pltpu.roll(gi, 1, 1, stride=1, stride_axis=0)[:, :BAND]
        if k == 0:
            sent[t] = rolled
        else:
            band[t % 3, k - 1] = rolled

    def exchange(t):
        return remote(sent.at[t], got.at[t], ex_s.at[t], ex_r.at[t], other, me_y)

    def ship(t):
        phase, s = t // SLABS, t % SLABS
        p, sl = s // PER, s % PER
        here = 1 - (lax.rem(p - me_y + PLANES, PLANES) + PLANES - 1) // PLANES
        here = here * (core if phase else 1 - core)
        base = (core * PLANES + me_y) * PER + sl
        at = base + here * (BLOCKS + sl - base)
        owner = chip * 2 + phase
        return remote(
            stage.at[t], out.at[at], out_s.at[t], out_r.at[at], owner + here * sign, p
        )

    def ship_here(sl):
        at = (core * PLANES + me_y) * PER + sl
        return pltpu.make_async_copy(
            stage.at[core * SLABS + me_y * PER + sl], out.at[at], c0_s.at[sl]
        )

    def factors(phase):
        first = chip * 8 + 4 * phase + me_y
        result = []
        for k, m in enumerate((0, 2, 3, 1)):
            e = first + offsets[k]
            scale = jnp.where((e >= 0) & (e < ENERGIES), -2.0, 0.0)
            result.append(scale * weights[m : m + 1, :])
        return result

    core_f = core.astype(F32)
    sign_f = sign.astype(F32)

    def finish(t, phase):
        s = t % SLABS
        fill = props[s // PER, 12 + s % PER]
        w = []
        for k, factor in enumerate(factors(phase)):
            w.append(factor * (core_f + sign_f * fill[phase * PICK + k : phase * PICK + k + 1]))
        slot = t % 3
        for i in range(ORB // 8):
            at = slice(8 * i, 8 * i + 8)
            x = sent[t, at] * w[0] + band[slot, 0, at] * w[1]
            x += band[slot, 1, at] * w[2] + got[t, at] * w[3]
            x = jnp.take_along_axis(x, flip8, axis=0)
            u = ORB // 8 - 1 - i
            stage[t, 8 * u : 8 * u + 8] = x

    def prop_rows(s, phase):
        p, sl = s // PER, s % PER
        at = slice(phase * PICK, phase * PICK + OWN)
        tiles = [props[p, 4 * sl + q][at] for q in range(4)]
        return jnp.concatenate(tiles[:2], axis=1), jnp.concatenate(tiles[2:], axis=1)

    def between(t):
        exchange(t).start()
        if t >= 1:
            exchange(t - 1).wait_recv()
        if t >= 2:
            ship(t - 2).start()
        if t + 1 < SLABS:
            ready(t + 1)
            if t + 3 < SLABS:
                forward(t + 3)

    for phase in range(2):
        real, imag = prop_rows(0, phase)
        for k in range(OWN):
            keep(
                k,
                phase * SLABS,
                jnp.where(anti, real[k : k + 1], 0.0),
                jnp.where(anti, imag[k : k + 1], 0.0),
            )
        if phase:
            finish(SLABS - 2, 0)
        between(phase * SLABS)

        def slab(s, phase=phase):
            t = phase * SLABS + s
            if phase == 0:
                c = cfull[s].astype(BF)
                ct = dot(dot_nt(flip, c).astype(BF), flip).astype(BF)
                cmat[s] = c
                ctmat[s] = ct
            c2 = jnp.concatenate([cmat[s], cmat[s]], axis=0)
            ct2 = jnp.concatenate([ctmat[s], ctmat[s]], axis=1)
            real, imag = prop_rows(s, phase)
            both = jnp.concatenate([real, imag, jnp.zeros((2, ORB), F32)], axis=0)
            columns = dot_nt(
                jnp.concatenate([flip, flip, flip], axis=1),
                jnp.concatenate(split3(both), axis=1),
            )

            def first(k):
                inner = dot(state[k], c2)
                high, low = split(inner)
                wide[k, 0, 0:ORB] = high[:ORB]
                wide[k, 0, ORB:] = low[:ORB]
                wide[k, 1, 0:ORB] = high[ORB:]
                wide[k, 1, ORB:] = low[ORB:]

            def second(k):
                hr = dot(ct2, wide[k, 0])
                hi = dot(ct2, wide[k, 1])
                rr = real[k : k + 1]
                ri = imag[k : k + 1]
                cr = columns[:, k : k + 1]
                ci = columns[:, OWN + k : OWN + k + 1]
                qr = hr * rr - hi * ri
                qi = hr * ri + hi * rr
                qr = jnp.where(anti, qr + 1.0, qr)
                keep(k, t, qr * cr - qi * ci, qr * ci + qi * cr)

            for k in range(OWN):
                first(k)
            if t >= 2:
                finish(t - 2, (t - 2) // SLABS)
            for k in range(OWN):
                second(k)
            between(t)

        for s in range(1, SLABS):
            slab(s)
    finish(STEPS - 2, 1)
    ship(STEPS - 2).start()
    exchange(STEPS - 1).wait_recv()
    finish(STEPS - 1, 1)
    ship(STEPS - 1).start()
    for sl in range(PER):
        ship_here(sl).start()

    for j in far_first:
        window(j).wait_send()
    for j in range(-NEAR, NEAR + 1):
        join(j).wait_send()
    for step in range(1, PLANES):
        pick_out(step).wait_send()

    @pl.when(me_y > 0)
    def _():
        coupling_sends(0, lambda c: c.wait_send())

    coupling_sends(1, lambda c: c.wait_send())
    coupling_sends(2, lambda c: c.wait_send())
    for i in range(1, ROW):
        @pl.when(me_y == 0)
        def _(i=i):
            coupling_here(0, i).wait()

    def passed(s, _):
        pass_on(s).wait_send()

        @pl.when(s // PER != me_y)
        def _():
            for i in range(1, ROW):
                coupling_beside(s, i).wait_send()

        return 0

    lax.fori_loop(1, SLABS, passed, 0)

    def shipped(t, _):
        exchange(t).wait_send()
        remote(stage.at[t], out.at[0], out_s.at[t], out_r.at[0], other, me_y).wait_send()
        return 0

    lax.fori_loop(0, STEPS, shipped, 0)

    def landed(i, _):
        @pl.when(i // PER != core * PLANES + me_y)
        def _():
            remote(stage.at[0], out.at[i], out_s.at[0], out_r.at[i], other, me_y).wait_recv()

        return 0

    lax.fori_loop(0, BLOCKS + PER, landed, 0)
    for sl in range(PER):
        ship_here(sl).wait()


def body(onsite, sigma_real, broadening, couplings, occupancy, mode_weights, mode_shifts):
    hbm = pl.BlockSpec(memory_space=pltpu.HBM)
    vmem = pltpu.VMEM
    dma = pltpu.SemaphoreType.DMA
    near = 2 * NEAR + 1
    out = pl.pallas_call(
        sweep_kernel,
        out_shape=jax.ShapeDtypeStruct((BLOCKS + PER, ORB, BAND), F32),
        in_specs=[hbm] * 7,
        out_specs=pl.BlockSpec(memory_space=pl.ANY),
        scratch_shapes=[
            pltpu.SMEM(mode_shifts.shape, jnp.int32),
            vmem(occupancy.shape, F32),
            vmem(onsite.shape, F32),
            vmem((PER, 4, ORB), F32),
            vmem((PER, 4, ORB), F32),
            vmem(couplings.shape, BF),
            vmem(mode_weights.shape, F32),
            vmem((PER, ORB, ORB), F32),
            vmem((8 * near, 16, HALF), F32),
            vmem((PLANES, 16, 8, HALF), F32),
            vmem((PLANES, 16, 8, HALF), F32),
            vmem((SLABS, ORB, ORB), F32),
            vmem((SLABS, ORB, ORB), BF),
            vmem((SLABS, ORB, ORB), BF),
            vmem((OWN, 2 * ORB, 2 * ORB), BF),
            vmem((OWN, 2, 2 * ORB, ORB), BF),
            vmem((STEPS, ORB, BAND), F32),
            vmem((STEPS, ORB, BAND), F32),
            vmem((3, OWN - 1, ORB, BAND), F32),
            vmem((STEPS, ORB, BAND), F32),
            dma((7,)),
            dma((near,)),
            dma((near,)),
            dma((near,)),
            dma((near,)),
            dma((PLANES,)),
            dma((PLANES,)),
            dma((PER,)),
            dma((PLANES - 1, PER)),
            dma((SLABS,)),
            dma((SLABS, ROW - 1)),
            dma((SLABS, ROW)),
            dma((SLABS,)),
            dma((SLABS,)),
            dma((STEPS,)),
            dma((STEPS,)),
            dma((STEPS,)),
            dma((BLOCKS + PER,)),
        ],
        compiler_params=pltpu.CompilerParams(
            collective_id=0, has_side_effects=True, vmem_limit_bytes=60 << 20
        ),
    )(
        mode_shifts,
        occupancy,
        onsite,
        jnp.swapaxes(sigma_real, 0, 1),
        jnp.swapaxes(broadening, 0, 1),
        couplings,
        mode_weights,
    )
    shape = (PLANES, PER, ORB, BAND)
    return out[:SLABS].reshape(shape), out[SLABS:BLOCKS].reshape(shape)


def solution(mesh):
    in_specs = (
        P("chain", None),
        P("energy", "chain", None),
        P("energy", "chain", None),
        P("chain", None, None),
        P("energy", "chain"),
        P(),
        P(),
    )
    out_specs = (P("energy", "chain", None, None), P("energy", "chain", None, None))
    return jax.shard_map(body, mesh=mesh, in_specs=in_specs, out_specs=out_specs, check_vma=False)
```

```python
import jax
import jax.numpy as jnp
from jax import lax
from jax.experimental import pallas as pl
from jax.experimental.pallas import tpu as pltpu
from jax.sharding import PartitionSpec as P

ORB = 256
HALF = 128
BAND = 128
SHIFT = 24
SLABS = 12
PLANES = 4
PER = 3
ENERGIES = 256
NEAR = 3
OWN = 3
PICK = 4
STEPS = 2 * SLABS
ROW = 4
PIECE = HALF // ROW
BLOCKS = 2 * PLANES * PER
RELAY = BLOCKS + PER
LAG = 6
EAGER = (1, 2, 21, 22, 23)
BF = jnp.bfloat16
F32 = jnp.float32
MESH = pl.DeviceIdType.MESH


def split(value):
    high = value.astype(BF)
    low = (value - high.astype(F32)).astype(BF)
    return high, low


def split3(value):
    high, rest = split(value)
    low = (value - high.astype(F32) - rest.astype(F32)).astype(BF)
    return high, rest, low


def dot(a, b):
    return jnp.dot(a, b, preferred_element_type=F32)


def dot_nt(a, b):
    return lax.dot_general(a, b, (((1,), (1,)), ((), ())), preferred_element_type=F32)


def sweep_kernel(
    shifts_in, filled_in, onsite_in, sigma_in, broadening_in, couplings_in, weights_in, out,
    shifts, filled, onsite, sigma_real, broadening, couplings, weights, cast,
    win, picked, props, cfull, cmat, ctmat, state, wide, sent, got, band, stage,
    in_s, win_s, win_r, join_s, join_r, pick_s, pick_r,
    c0_s, c1_s, c1_r, c2_s, c2_r, c3_s, c3_r, ex_s, ex_r, out_s, out_r, relay_s,
):
    loads = [
        pltpu.make_async_copy(source, target, in_s.at[i])
        for i, (source, target) in enumerate(
            (
                (couplings_in, couplings),
                (onsite_in, onsite),
                (sigma_in, sigma_real),
                (broadening_in, broadening),
                (filled_in, filled),
                (weights_in, weights),
                (shifts_in, shifts),
            )
        )
    ]
    for load in loads:
        load.start()

    me_e = lax.axis_index("energy")
    me_y = lax.axis_index("chain")
    devices = lax.axis_size("energy")
    chips = devices // 2
    chip = me_e // 2
    core = lax.rem(me_e, 2)
    sign = 1 - 2 * core
    other = me_e + sign
    me_x = me_e // (devices // ROW)

    rows = lax.broadcasted_iota(jnp.int32, (ORB, ORB), 0)
    cols = lax.broadcasted_iota(jnp.int32, (ORB, ORB), 1)
    anti = rows + cols == ORB - 1
    flip = jnp.where(anti, 1.0, 0.0).astype(BF)
    flip8 = 7 - lax.broadcasted_iota(jnp.int32, (8, BAND), 0)

    def near(j):
        return lax.rem(chip + j + chips, chips) * 2 + core

    def beside(i):
        return lax.rem(me_e + i * (devices // ROW), devices)

    def plane(step):
        return lax.rem(me_y + step, PLANES)

    def remote(source, target, send_sem, recv_sem, e, y):
        return pltpu.make_async_remote_copy(
            src_ref=source,
            dst_ref=target,
            send_sem=send_sem,
            recv_sem=recv_sem,
            device_id=(e, y),
            device_id_type=MESH,
        )

    barrier = pltpu.get_barrier_semaphore()
    peers = [(near(j), me_y) for j in range(-NEAR, NEAR + 1) if j]
    peers += [(beside(i), me_y) for i in range(1, ROW)]
    peers += [(me_e, plane(step)) for step in range(1, PLANES)]
    peers += [(other, plane(step)) for step in range(PLANES)]
    for peer in peers:
        pl.semaphore_signal(barrier, inc=1, device_id=peer, device_id_type=MESH)

    mine = (2 * NEAR + core) * 4
    for load in loads[1:]:
        load.wait()
    points = (me_e * 4 + lax.broadcasted_iota(jnp.int32, (4, ORB), 0)).astype(F32)
    energy = -3.0 + 6.0 * (points + 0.5) / ENERGIES
    for sl in range(PER):
        detuning = energy - onsite[sl : sl + 1] - sigma_real[sl]
        width = broadening[sl]
        scale = detuning * detuning + width * width
        real = detuning / scale
        imag = -width / scale
        for i in range(4):
            for h in range(2):
                lanes = slice(HALF * h, HALF * (h + 1))
                win[mine + i, 4 * sl + h : 4 * sl + h + 1] = real[i : i + 1, lanes]
                win[mine + i, 4 * sl + 2 + h : 4 * sl + 3 + h] = imag[i : i + 1, lanes]
            win[mine + i, 12 + sl : 13 + sl] = jnp.broadcast_to(filled[i : i + 1, sl : sl + 1], (1, HALF))
    for i in range(4):
        win[mine + i, 15:16] = jnp.zeros((1, HALF), F32)

    loads[0].wait()
    for j in range(PER):
        cast[j] = couplings[j].astype(F32)

    pl.semaphore_wait(barrier, len(peers))

    def window(j):
        return remote(
            win.at[pl.ds(mine, 4)],
            win.at[pl.ds(((NEAR - j) * 2 + core) * 4, 4)],
            win_s.at[j + NEAR],
            win_r.at[NEAR - j],
            near(j),
            me_y,
        )

    def join(j):
        part = win.at[pl.ds(((NEAR + j) * 2 + core) * 4, 4)]
        return remote(part, part, join_s.at[j + NEAR], join_r.at[j + NEAR], other, me_y)

    def joined(j):
        part = win.at[pl.ds(((NEAR + j) * 2 + 1 - core) * 4, 4)]
        return remote(part, part, join_s.at[j + NEAR], join_r.at[j + NEAR], other, me_y)

    far_first = (3, -3, 2, -2, 1, -1)
    for j in far_first:
        window(j).start()
    join(0).start()

    piece = core * HALF + me_x * PIECE

    def part_of(s, x):
        return cfull.at[s, pl.ds(core * HALF + x * PIECE, PIECE)]

    def coupling_out(step, j):
        s = me_y * PER + j
        return remote(
            cast.at[j, pl.ds(piece, PIECE)],
            part_of(s, me_x),
            c1_s.at[step - 1, j],
            c1_r.at[s],
            me_e,
            plane(step),
        )

    def coupling_sends(j, act):
        for step in (1, 3, 2):
            act(coupling_out(step, j))

    @pl.when(me_y > 0)
    def _():
        coupling_sends(0, lambda c: c.start())

    coupling_sends(1, lambda c: c.start())
    coupling_sends(2, lambda c: c.start())

    def coupling_here(j, i):
        x = lax.rem(me_x + i, ROW)
        s = me_y * PER + j
        sem = c2_r.at[s, x] if i else c0_s.at[j]
        return pltpu.make_async_copy(
            cast.at[j, pl.ds(core * HALF + x * PIECE, PIECE)], part_of(s, x), sem
        )

    for j in range(PER):
        for i in range(ROW):
            coupling_here(j, i).start()

    def coupling_beside(s, i):
        part = part_of(s, me_x)
        return remote(part, part, c2_s.at[s, i - 1], c2_r.at[s, me_x], beside(i), me_y)

    for s in (1, 3, 6, 9, 2, 4, 7, 10, 5, 8, 11):
        @pl.when(s // PER != me_y)
        def _(s=s):
            part = part_of(s, me_x)
            remote(part, part, c1_s.at[0, 0], c1_r.at[s], me_e, s // PER).wait_recv()
            for i in (1, 3, 2):
                coupling_beside(s, i).start()

    for j in far_first[::-1]:
        part = win.at[pl.ds(((NEAR + j) * 2 + core) * 4, 4)]
        remote(part, part, win_s.at[0], win_r.at[NEAR + j], other, me_y).wait_recv()
        join(j).start()
    for j in (0,) + far_first[::-1]:
        joined(j).wait_recv()

    s2 = shifts[2] * sign
    s3 = shifts[3] * sign
    offsets = (SHIFT * sign, s2, s3, -SHIFT * sign)
    for y in range(PLANES):
        for phase in range(2):
            for k in range(PICK):
                value = win[SHIFT + 4 * phase + y + offsets[k]]
                picked[y, :, phase * PICK + k, :] = value

    def pick_out(step):
        return remote(
            picked.at[plane(step)],
            props.at[me_y],
            pick_s.at[step],
            pick_r.at[me_y],
            me_e,
            plane(step),
        )

    pick_here = pltpu.make_async_copy(picked.at[me_y], props.at[me_y], pick_s.at[0])
    for step in (2, 1, 3):
        pick_out(step).start()
    pick_here.start()

    def pass_on(s):
        part = cfull.at[s, pl.ds(core * HALF, HALF)]
        return remote(part, part, c3_s.at[s], c3_r.at[s], other, me_y)

    def forward(s):
        for i in range(1, ROW):
            x = lax.rem(me_x + i, ROW)
            part = part_of(s, x)
            remote(part, part, c1_s.at[0, 0], c2_r.at[s, x], other, me_y).wait_recv()
        pass_on(s).start()

    def ready(s):
        part = cfull.at[s, pl.ds((1 - core) * HALF, HALF)]
        remote(part, part, c3_s.at[s], c3_r.at[s], other, me_y).wait_recv()

    for j in range(PER):
        coupling_here(j, 0).wait()
    forward(1)
    forward(2)

    pick_here.wait()
    for step in range(1, PLANES):
        source = plane(step)
        remote(
            picked.at[0], props.at[source], pick_s.at[step], pick_r.at[source], me_e, source
        ).wait_recv()

    def keep(k, t, gr, gi):
        high, low = split(gr)
        state[k, 0:ORB, 0:ORB] = high
        state[k, 0:ORB, ORB:] = low
        high, low = split(gi)
        state[k, ORB:, 0:ORB] = high
        state[k, ORB:, ORB:] = low
        rolled = pltpu.roll(gi, 1, 1, stride=1, stride_axis=0)[:, :BAND]
        if k == 0:
            sent[t] = rolled
        else:
            band[t % 3, k - 1] = rolled

    def exchange(t):
        return remote(sent.at[t], got.at[t], ex_s.at[t], ex_r.at[t], other, me_y)

    def ship(t):
        phase, s = t // SLABS, t % SLABS
        p, sl = s // PER, s % PER
        away = lax.rem(p - me_y + PLANES, PLANES)
        here = 1 - (away + PLANES - 1) // PLANES
        here = here * (core if phase else 1 - core)
        relay = (away // 2) * (1 - lax.rem(away, 2)) * (1 - core)
        base = (core * PLANES + me_y) * PER + sl
        at = base + here * (BLOCKS + sl - base) + relay * (RELAY + phase * PER + sl - base)
        owner = chip * 2 + phase
        return remote(
            stage.at[t],
            out.at[at],
            out_s.at[t],
            out_r.at[at],
            owner + here * sign + relay * (me_e - owner),
            p + relay * (PLANES - 1 - me_y - p),
        )

    def relayed(t):
        phase, sl = t // SLABS, t % PER
        at = (PLANES - 1 - me_y) * PER + sl
        return remote(
            out.at[RELAY + phase * PER + sl],
            out.at[at],
            relay_s.at[phase * PER + sl],
            out_r.at[at],
            chip * 2 + phase,
            lax.rem(PLANES + 1 - me_y, PLANES),
        )

    def relaying(t, act):
        @pl.when((core == 0) & (lax.rem(PLANES + 1 - me_y, PLANES) == t % SLABS // PER))
        def _():
            act(t)

    def relay_on(t):
        phase, sl = t // SLABS, t % PER
        at = RELAY + phase * PER + sl
        remote(
            out.at[at], out.at[at], relay_s.at[0], out_r.at[at], me_e, PLANES - 1 - me_y
        ).wait_recv()
        relayed(t).start()

    def ship_here(sl):
        at = (core * PLANES + me_y) * PER + sl
        return pltpu.make_async_copy(
            stage.at[core * SLABS + me_y * PER + sl], out.at[at], c0_s.at[sl]
        )

    def factors(phase):
        first = chip * 8 + 4 * phase + me_y
        result = []
        for k, m in enumerate((0, 2, 3, 1)):
            e = first + offsets[k]
            scale = jnp.where((e >= 0) & (e < ENERGIES), -2.0, 0.0)
            result.append(scale * weights[m : m + 1, :])
        return result

    core_f = core.astype(F32)
    sign_f = sign.astype(F32)

    def finish(t, phase):
        s = t % SLABS
        fill = props[s // PER, 12 + s % PER]
        w = []
        for k, factor in enumerate(factors(phase)):
            w.append(factor * (core_f + sign_f * fill[phase * PICK + k : phase * PICK + k + 1]))
        slot = t % 3
        for i in range(ORB // 8):
            at = slice(8 * i, 8 * i + 8)
            x = sent[t, at] * w[0] + band[slot, 0, at] * w[1]
            x += band[slot, 1, at] * w[2] + got[t, at] * w[3]
            x = jnp.take_along_axis(x, flip8, axis=0)
            u = ORB // 8 - 1 - i
            stage[t, 8 * u : 8 * u + 8] = x

    def prop_rows(s, phase):
        p, sl = s // PER, s % PER
        at = slice(phase * PICK, phase * PICK + OWN)
        tiles = [props[p, 4 * sl + q][at] for q in range(4)]
        return jnp.concatenate(tiles[:2], axis=1), jnp.concatenate(tiles[2:], axis=1)

    def between(t):
        exchange(t).start()
        if t >= 1:
            exchange(t - 1).wait_recv()
        if t >= 2 and t - 1 not in EAGER:
            ship(t - 2).start()
        if t + 1 < SLABS:
            ready(t + 1)
            if t + 3 < SLABS:
                forward(t + 3)
        if t >= LAG:
            relaying(t - LAG, relay_on)
        if t in EAGER:
            finish(t - 1, (t - 1) // SLABS)
            ship(t - 1).start()

    for phase in range(2):
        real, imag = prop_rows(0, phase)
        for k in range(OWN):
            keep(
                k,
                phase * SLABS,
                jnp.where(anti, real[k : k + 1], 0.0),
                jnp.where(anti, imag[k : k + 1], 0.0),
            )
        if phase:
            finish(SLABS - 2, 0)
        between(phase * SLABS)

        def slab(s, phase=phase):
            t = phase * SLABS + s
            if phase == 0:
                c = cfull[s].astype(BF)
                ct = dot(dot_nt(flip, c).astype(BF), flip).astype(BF)
                cmat[s] = c
                ctmat[s] = ct
            c2 = jnp.concatenate([cmat[s], cmat[s]], axis=0)
            ct2 = jnp.concatenate([ctmat[s], ctmat[s]], axis=1)
            real, imag = prop_rows(s, phase)
            both = jnp.concatenate([real, imag, jnp.zeros((2, ORB), F32)], axis=0)
            columns = dot_nt(
                jnp.concatenate([flip, flip, flip], axis=1),
                jnp.concatenate(split3(both), axis=1),
            )

            def first(k):
                inner = dot(state[k], c2)
                high, low = split(inner)
                wide[k, 0, 0:ORB] = high[:ORB]
                wide[k, 0, ORB:] = low[:ORB]
                wide[k, 1, 0:ORB] = high[ORB:]
                wide[k, 1, ORB:] = low[ORB:]

            def second(k):
                hr = dot(ct2, wide[k, 0])
                hi = dot(ct2, wide[k, 1])
                rr = real[k : k + 1]
                ri = imag[k : k + 1]
                cr = columns[:, k : k + 1]
                ci = columns[:, OWN + k : OWN + k + 1]
                qr = hr * rr - hi * ri
                qi = hr * ri + hi * rr
                qr = jnp.where(anti, qr + 1.0, qr)
                keep(k, t, qr * cr - qi * ci, qr * ci + qi * cr)

            for k in range(OWN):
                first(k)
            if t >= 2 and t - 1 not in EAGER:
                finish(t - 2, (t - 2) // SLABS)
            for k in range(OWN):
                second(k)
            between(t)

        for s in range(1, SLABS):
            slab(s)
    exchange(STEPS - 1).wait_recv()
    finish(STEPS - 1, 1)
    ship(STEPS - 1).start()
    for t in range(STEPS - LAG, STEPS):
        relaying(t, relay_on)
    for sl in range(PER):
        ship_here(sl).start()

    for j in far_first:
        window(j).wait_send()
    for j in range(-NEAR, NEAR + 1):
        join(j).wait_send()
    for step in range(1, PLANES):
        pick_out(step).wait_send()

    @pl.when(me_y > 0)
    def _():
        coupling_sends(0, lambda c: c.wait_send())

    coupling_sends(1, lambda c: c.wait_send())
    coupling_sends(2, lambda c: c.wait_send())
    for i in range(1, ROW):
        @pl.when(me_y == 0)
        def _(i=i):
            coupling_here(0, i).wait()

    def passed(s, _):
        pass_on(s).wait_send()

        @pl.when(s // PER != me_y)
        def _():
            for i in range(1, ROW):
                coupling_beside(s, i).wait_send()

        return 0

    lax.fori_loop(1, SLABS, passed, 0)

    def shipped(t, _):
        exchange(t).wait_send()
        remote(stage.at[t], out.at[0], out_s.at[t], out_r.at[0], other, me_y).wait_send()
        return 0

    lax.fori_loop(0, STEPS, shipped, 0)
    for t in range(STEPS):
        relaying(t, lambda t: relayed(t).wait_send())

    def landed(i, _):
        @pl.when(i // PER != core * PLANES + me_y)
        def _():
            remote(stage.at[0], out.at[i], out_s.at[0], out_r.at[i], other, me_y).wait_recv()

        return 0

    lax.fori_loop(0, RELAY, landed, 0)
    for sl in range(PER):
        ship_here(sl).wait()


def body(onsite, sigma_real, broadening, couplings, occupancy, mode_weights, mode_shifts):
    hbm = pl.BlockSpec(memory_space=pltpu.HBM)
    vmem = pltpu.VMEM
    dma = pltpu.SemaphoreType.DMA
    near = 2 * NEAR + 1
    out = pl.pallas_call(
        sweep_kernel,
        out_shape=jax.ShapeDtypeStruct((RELAY + 2 * PER, ORB, BAND), F32),
        in_specs=[hbm] * 7,
        out_specs=pl.BlockSpec(memory_space=pl.ANY),
        scratch_shapes=[
            pltpu.SMEM(mode_shifts.shape, jnp.int32),
            vmem(occupancy.shape, F32),
            vmem(onsite.shape, F32),
            vmem((PER, 4, ORB), F32),
            vmem((PER, 4, ORB), F32),
            vmem(couplings.shape, BF),
            vmem(mode_weights.shape, F32),
            vmem((PER, ORB, ORB), F32),
            vmem((8 * near, 16, HALF), F32),
            vmem((PLANES, 16, 8, HALF), F32),
            vmem((PLANES, 16, 8, HALF), F32),
            vmem((SLABS, ORB, ORB), F32),
            vmem((SLABS, ORB, ORB), BF),
            vmem((SLABS, ORB, ORB), BF),
            vmem((OWN, 2 * ORB, 2 * ORB), BF),
            vmem((OWN, 2, 2 * ORB, ORB), BF),
            vmem((STEPS, ORB, BAND), F32),
            vmem((STEPS, ORB, BAND), F32),
            vmem((3, OWN - 1, ORB, BAND), F32),
            vmem((STEPS, ORB, BAND), F32),
            dma((7,)),
            dma((near,)),
            dma((near,)),
            dma((near,)),
            dma((near,)),
            dma((PLANES,)),
            dma((PLANES,)),
            dma((PER,)),
            dma((PLANES - 1, PER)),
            dma((SLABS,)),
            dma((SLABS, ROW - 1)),
            dma((SLABS, ROW)),
            dma((SLABS,)),
            dma((SLABS,)),
            dma((STEPS,)),
            dma((STEPS,)),
            dma((STEPS,)),
            dma((RELAY + 2 * PER,)),
            dma((2 * PER,)),
        ],
        compiler_params=pltpu.CompilerParams(
            collective_id=0, has_side_effects=True, vmem_limit_bytes=60 << 20
        ),
    )(
        mode_shifts,
        occupancy,
        onsite,
        jnp.swapaxes(sigma_real, 0, 1),
        jnp.swapaxes(broadening, 0, 1),
        couplings,
        mode_weights,
    )
    shape = (PLANES, PER, ORB, BAND)
    return out[:SLABS].reshape(shape), out[SLABS:BLOCKS].reshape(shape)


def solution(mesh):
    in_specs = (
        P("chain", None),
        P("energy", "chain", None),
        P("energy", "chain", None),
        P("chain", None, None),
        P("energy", "chain"),
        P(),
        P(),
    )
    out_specs = (P("energy", "chain", None, None), P("energy", "chain", None, None))
    return jax.shard_map(body, mesh=mesh, in_specs=in_specs, out_specs=out_specs, check_vma=False)
```

```python
import jax
import jax.numpy as jnp
from jax import lax
from jax.experimental import pallas as pl
from jax.experimental.pallas import tpu as pltpu
from jax.sharding import PartitionSpec as P

ORB = 256
HALF = 128
BAND = 128
SHIFT = 24
SLABS = 12
PLANES = 4
PER = 3
ENERGIES = 256
NEAR = 3
OWN = 3
PICK = 4
STEPS = 2 * SLABS
ROW = 4
PIECE = HALF // ROW
BLOCKS = 2 * PLANES * PER
AHEAD = 3
GROUPS = ((0,), (1,)) + tuple((t, t + 1) for t in range(2, 22, 2)) + ((22,), (23,))
BF = jnp.bfloat16
F32 = jnp.float32
MESH = pl.DeviceIdType.MESH


def split(value):
    high = value.astype(BF)
    low = (value - high.astype(F32)).astype(BF)
    return high, low


def split3(value):
    high, rest = split(value)
    low = (value - high.astype(F32) - rest.astype(F32)).astype(BF)
    return high, rest, low


def dot(a, b):
    return jnp.dot(a, b, preferred_element_type=F32)


def dot_nt(a, b):
    return lax.dot_general(a, b, (((1,), (1,)), ((), ())), preferred_element_type=F32)


def sweep_kernel(
    shifts_in, filled_in, onsite_in, sigma_in, broadening_in, couplings_in, weights_in, out,
    shifts, filled, onsite, sigma_real, broadening, couplings, weights, cast,
    win, picked, props, cfull, cmat, ctmat, state, wide, sent, got, band, stage,
    in_s, win_s, win_r, join_s, join_r, pick_s, pick_r,
    c0_s, c1_s, c1_r, c2_s, c2_r, c3_s, c3_r, ex_s, ex_r, out_s, out_r,
):
    loads = [
        pltpu.make_async_copy(source, target, in_s.at[i])
        for i, (source, target) in enumerate(
            (
                (couplings_in, couplings),
                (onsite_in, onsite),
                (sigma_in, sigma_real),
                (broadening_in, broadening),
                (filled_in, filled),
                (weights_in, weights),
                (shifts_in, shifts),
            )
        )
    ]
    for load in loads:
        load.start()

    me_e = lax.axis_index("energy")
    me_y = lax.axis_index("chain")
    devices = lax.axis_size("energy")
    chips = devices // 2
    chip = me_e // 2
    core = lax.rem(me_e, 2)
    sign = 1 - 2 * core
    other = me_e + sign
    me_x = me_e // (devices // ROW)

    rows = lax.broadcasted_iota(jnp.int32, (ORB, ORB), 0)
    cols = lax.broadcasted_iota(jnp.int32, (ORB, ORB), 1)
    anti = rows + cols == ORB - 1
    flip = jnp.where(anti, 1.0, 0.0).astype(BF)
    flip8 = 7 - lax.broadcasted_iota(jnp.int32, (8, BAND), 0)

    def near(j):
        return lax.rem(chip + j + chips, chips) * 2 + core

    def beside(i):
        return lax.rem(me_e + i * (devices // ROW), devices)

    def plane(step):
        return lax.rem(me_y + step, PLANES)

    def remote(source, target, send_sem, recv_sem, e, y):
        return pltpu.make_async_remote_copy(
            src_ref=source,
            dst_ref=target,
            send_sem=send_sem,
            recv_sem=recv_sem,
            device_id=(e, y),
            device_id_type=MESH,
        )

    barrier = pltpu.get_barrier_semaphore()
    peers = [(near(j), me_y) for j in range(-NEAR, NEAR + 1) if j]
    peers += [(beside(i), me_y) for i in range(1, ROW)]
    peers += [(me_e, plane(step)) for step in range(1, PLANES)]
    peers += [(other, plane(step)) for step in range(PLANES)]
    for peer in peers:
        pl.semaphore_signal(barrier, inc=1, device_id=peer, device_id_type=MESH)

    mine = (2 * NEAR + core) * 4
    for load in loads[1:]:
        load.wait()
    points = (me_e * 4 + lax.broadcasted_iota(jnp.int32, (4, ORB), 0)).astype(F32)
    energy = -3.0 + 6.0 * (points + 0.5) / ENERGIES
    for sl in range(PER):
        detuning = energy - onsite[sl : sl + 1] - sigma_real[sl]
        width = broadening[sl]
        scale = detuning * detuning + width * width
        real = detuning / scale
        imag = -width / scale
        for i in range(4):
            for h in range(2):
                lanes = slice(HALF * h, HALF * (h + 1))
                win[mine + i, 4 * sl + h : 4 * sl + h + 1] = real[i : i + 1, lanes]
                win[mine + i, 4 * sl + 2 + h : 4 * sl + 3 + h] = imag[i : i + 1, lanes]
            win[mine + i, 12 + sl : 13 + sl] = jnp.broadcast_to(filled[i : i + 1, sl : sl + 1], (1, HALF))
    for i in range(4):
        win[mine + i, 15:16] = jnp.zeros((1, HALF), F32)

    loads[0].wait()
    for j in range(PER):
        cast[j] = couplings[j].astype(F32)

    pl.semaphore_wait(barrier, len(peers))

    def window(j):
        return remote(
            win.at[pl.ds(mine, 4)],
            win.at[pl.ds(((NEAR - j) * 2 + core) * 4, 4)],
            win_s.at[j + NEAR],
            win_r.at[NEAR - j],
            near(j),
            me_y,
        )

    def join(j):
        part = win.at[pl.ds(((NEAR + j) * 2 + core) * 4, 4)]
        return remote(part, part, join_s.at[j + NEAR], join_r.at[j + NEAR], other, me_y)

    def joined(j):
        part = win.at[pl.ds(((NEAR + j) * 2 + 1 - core) * 4, 4)]
        return remote(part, part, join_s.at[j + NEAR], join_r.at[j + NEAR], other, me_y)

    far_first = (3, -3, 2, -2, 1, -1)
    for j in far_first:
        window(j).start()
    join(0).start()

    piece = core * HALF + me_x * PIECE

    def part_of(s, x):
        return cfull.at[s, pl.ds(core * HALF + x * PIECE, PIECE)]

    def coupling_out(step, j):
        s = me_y * PER + j
        return remote(
            cast.at[j, pl.ds(piece, PIECE)],
            part_of(s, me_x),
            c1_s.at[step - 1, j],
            c1_r.at[s],
            me_e,
            plane(step),
        )

    def coupling_sends(j, act):
        for step in (1, 3, 2):
            act(coupling_out(step, j))

    @pl.when(me_y > 0)
    def _():
        coupling_sends(0, lambda c: c.start())

    coupling_sends(1, lambda c: c.start())
    coupling_sends(2, lambda c: c.start())

    def coupling_here(j, i):
        x = lax.rem(me_x + i, ROW)
        s = me_y * PER + j
        sem = c2_r.at[s, x] if i else c0_s.at[j]
        return pltpu.make_async_copy(
            cast.at[j, pl.ds(core * HALF + x * PIECE, PIECE)], part_of(s, x), sem
        )

    for j in range(PER):
        for i in range(ROW):
            coupling_here(j, i).start()

    def coupling_beside(s, i):
        part = part_of(s, me_x)
        return remote(part, part, c2_s.at[s, i - 1], c2_r.at[s, me_x], beside(i), me_y)

    for s in (1, 3, 6, 9, 2, 4, 7, 10, 5, 8, 11):
        @pl.when(s // PER != me_y)
        def _(s=s):
            part = part_of(s, me_x)
            remote(part, part, c1_s.at[0, 0], c1_r.at[s], me_e, s // PER).wait_recv()
            for i in (1, 3, 2):
                coupling_beside(s, i).start()

    for j in far_first[::-1]:
        part = win.at[pl.ds(((NEAR + j) * 2 + core) * 4, 4)]
        remote(part, part, win_s.at[0], win_r.at[NEAR + j], other, me_y).wait_recv()
        join(j).start()
    for j in (0,) + far_first[::-1]:
        joined(j).wait_recv()

    s2 = shifts[2] * sign
    s3 = shifts[3] * sign
    offsets = (SHIFT * sign, s2, s3, -SHIFT * sign)
    for y in range(PLANES):
        for phase in range(2):
            for k in range(PICK):
                value = win[SHIFT + 4 * phase + y + offsets[k]]
                picked[y, :, phase * PICK + k, :] = value

    def pick_out(step):
        return remote(
            picked.at[plane(step)],
            props.at[me_y],
            pick_s.at[step],
            pick_r.at[me_y],
            me_e,
            plane(step),
        )

    pick_here = pltpu.make_async_copy(picked.at[me_y], props.at[me_y], pick_s.at[0])
    for step in (2, 1, 3):
        pick_out(step).start()
    pick_here.start()

    def pass_on(s):
        part = cfull.at[s, pl.ds(core * HALF, HALF)]
        return remote(part, part, c3_s.at[s], c3_r.at[s], other, me_y)

    def forward(s):
        for i in range(1, ROW):
            x = lax.rem(me_x + i, ROW)
            part = part_of(s, x)
            remote(part, part, c1_s.at[0, 0], c2_r.at[s, x], other, me_y).wait_recv()
        pass_on(s).start()

    def ready(s):
        part = cfull.at[s, pl.ds((1 - core) * HALF, HALF)]
        remote(part, part, c3_s.at[s], c3_r.at[s], other, me_y).wait_recv()

    for j in range(PER):
        coupling_here(j, 0).wait()
    for s in range(1, AHEAD + 1):
        forward(s)

    pick_here.wait()
    for step in range(1, PLANES):
        source = plane(step)
        remote(
            picked.at[0], props.at[source], pick_s.at[step], pick_r.at[source], me_e, source
        ).wait_recv()

    def keep(k, t, gr, gi):
        high, low = split(gr)
        state[k, 0:ORB, 0:ORB] = high
        state[k, 0:ORB, ORB:] = low
        high, low = split(gi)
        state[k, ORB:, 0:ORB] = high
        state[k, ORB:, ORB:] = low
        rolled = pltpu.roll(gi, 1, 1, stride=1, stride_axis=0)[:, :BAND]
        if k == 0:
            sent[t] = rolled
        else:
            band[t % 4, k - 1] = rolled

    def exchange(t):
        return remote(sent.at[t], got.at[t], ex_s.at[t], ex_r.at[t], other, me_y)

    def ship(t):
        phase, s = t // SLABS, t % SLABS
        p, sl = s // PER, s % PER
        here = 1 - (lax.rem(p - me_y + PLANES, PLANES) + PLANES - 1) // PLANES
        here = here * (core if phase else 1 - core)
        base = (core * PLANES + me_y) * PER + sl
        at = base + here * (BLOCKS + sl - base)
        owner = chip * 2 + phase
        return remote(
            stage.at[t], out.at[at], out_s.at[t], out_r.at[at], owner + here * sign, p
        )

    def ship_here(sl):
        at = (core * PLANES + me_y) * PER + sl
        return pltpu.make_async_copy(
            stage.at[core * SLABS + me_y * PER + sl], out.at[at], c0_s.at[sl]
        )

    def factors(phase):
        first = chip * 8 + 4 * phase + me_y
        result = []
        for k, m in enumerate((0, 2, 3, 1)):
            e = first + offsets[k]
            scale = jnp.where((e >= 0) & (e < ENERGIES), -2.0, 0.0)
            result.append(scale * weights[m : m + 1, :])
        return result

    core_f = core.astype(F32)
    sign_f = sign.astype(F32)

    def finish(t, phase):
        s = t % SLABS
        fill = props[s // PER, 12 + s % PER]
        w = []
        for k, factor in enumerate(factors(phase)):
            w.append(factor * (core_f + sign_f * fill[phase * PICK + k : phase * PICK + k + 1]))
        slot = t % 4
        for i in range(ORB // 8):
            at = slice(8 * i, 8 * i + 8)
            x = sent[t, at] * w[0] + band[slot, 0, at] * w[1]
            x += band[slot, 1, at] * w[2] + got[t, at] * w[3]
            x = jnp.take_along_axis(x, flip8, axis=0)
            u = ORB // 8 - 1 - i
            stage[t, 8 * u : 8 * u + 8] = x

    def prop_rows(s, phase):
        p, sl = s // PER, s % PER
        at = slice(phase * PICK, phase * PICK + OWN)
        tiles = [props[p, 4 * sl + q][at] for q in range(4)]
        return jnp.concatenate(tiles[:2], axis=1), jnp.concatenate(tiles[2:], axis=1)

    def start(phase):
        real, imag = prop_rows(0, phase)
        for k in range(OWN):
            keep(
                k,
                phase * SLABS,
                jnp.where(anti, real[k : k + 1], 0.0),
                jnp.where(anti, imag[k : k + 1], 0.0),
            )

    def slab(s, phase):
        t = phase * SLABS + s
        if phase == 0:
            c = cfull[s].astype(BF)
            ct = dot(dot_nt(flip, c).astype(BF), flip).astype(BF)
            cmat[s] = c
            ctmat[s] = ct
        c2 = jnp.concatenate([cmat[s], cmat[s]], axis=0)
        ct2 = jnp.concatenate([ctmat[s], ctmat[s]], axis=1)
        real, imag = prop_rows(s, phase)
        both = jnp.concatenate([real, imag, jnp.zeros((2, ORB), F32)], axis=0)
        columns = dot_nt(
            jnp.concatenate([flip, flip, flip], axis=1),
            jnp.concatenate(split3(both), axis=1),
        )

        def first(k):
            inner = dot(state[k], c2)
            high, low = split(inner)
            wide[k, 0, 0:ORB] = high[:ORB]
            wide[k, 0, ORB:] = low[:ORB]
            wide[k, 1, 0:ORB] = high[ORB:]
            wide[k, 1, ORB:] = low[ORB:]

        def second(k):
            hr = dot(ct2, wide[k, 0])
            hi = dot(ct2, wide[k, 1])
            rr = real[k : k + 1]
            ri = imag[k : k + 1]
            cr = columns[:, k : k + 1]
            ci = columns[:, OWN + k : OWN + k + 1]
            qr = hr * rr - hi * ri
            qi = hr * ri + hi * rr
            qr = jnp.where(anti, qr + 1.0, qr)
            keep(k, t, qr * cr - qi * ci, qr * ci + qi * cr)

        for k in range(OWN):
            first(k)
        for k in range(OWN):
            second(k)

    def conclude(group):
        for t in group:
            exchange(t).wait_recv()
        for t in group:
            finish(t, t // SLABS)
            ship(t).start()

    for i, group in enumerate(GROUPS):
        for t in group:
            if t % SLABS:
                slab(t % SLABS, t // SLABS)
            else:
                start(t // SLABS)
        for t in group:
            exchange(t).start()
        after = GROUPS[i + 1] if i + 1 < len(GROUPS) else ()
        for t in after:
            if t < SLABS:
                ready(t)
        for t in GROUPS[i + 2] if i + 2 < len(GROUPS) else ():
            if AHEAD < t < SLABS:
                forward(t)
        if i:
            conclude(GROUPS[i - 1])
    conclude(GROUPS[-1])

    for sl in range(PER):
        ship_here(sl).start()

    for j in far_first:
        window(j).wait_send()
    for j in range(-NEAR, NEAR + 1):
        join(j).wait_send()
    for step in range(1, PLANES):
        pick_out(step).wait_send()

    @pl.when(me_y > 0)
    def _():
        coupling_sends(0, lambda c: c.wait_send())

    coupling_sends(1, lambda c: c.wait_send())
    coupling_sends(2, lambda c: c.wait_send())
    for i in range(1, ROW):
        @pl.when(me_y == 0)
        def _(i=i):
            coupling_here(0, i).wait()

    def passed(s, _):
        pass_on(s).wait_send()

        @pl.when(s // PER != me_y)
        def _():
            for i in range(1, ROW):
                coupling_beside(s, i).wait_send()

        return 0

    lax.fori_loop(1, SLABS, passed, 0)

    def shipped(t, _):
        exchange(t).wait_send()
        remote(stage.at[t], out.at[0], out_s.at[t], out_r.at[0], other, me_y).wait_send()
        return 0

    lax.fori_loop(0, STEPS, shipped, 0)

    def landed(i, _):
        @pl.when(i // PER != core * PLANES + me_y)
        def _():
            remote(stage.at[0], out.at[i], out_s.at[0], out_r.at[i], other, me_y).wait_recv()

        return 0

    lax.fori_loop(0, BLOCKS + PER, landed, 0)
    for sl in range(PER):
        ship_here(sl).wait()


def body(onsite, sigma_real, broadening, couplings, occupancy, mode_weights, mode_shifts):
    hbm = pl.BlockSpec(memory_space=pltpu.HBM)
    vmem = pltpu.VMEM
    dma = pltpu.SemaphoreType.DMA
    near = 2 * NEAR + 1
    out = pl.pallas_call(
        sweep_kernel,
        out_shape=jax.ShapeDtypeStruct((BLOCKS + PER, ORB, BAND), F32),
        in_specs=[hbm] * 7,
        out_specs=pl.BlockSpec(memory_space=pl.ANY),
        scratch_shapes=[
            pltpu.SMEM(mode_shifts.shape, jnp.int32),
            vmem(occupancy.shape, F32),
            vmem(onsite.shape, F32),
            vmem((PER, 4, ORB), F32),
            vmem((PER, 4, ORB), F32),
            vmem(couplings.shape, BF),
            vmem(mode_weights.shape, F32),
            vmem((PER, ORB, ORB), F32),
            vmem((8 * near, 16, HALF), F32),
            vmem((PLANES, 16, 8, HALF), F32),
            vmem((PLANES, 16, 8, HALF), F32),
            vmem((SLABS, ORB, ORB), F32),
            vmem((SLABS, ORB, ORB), BF),
            vmem((SLABS, ORB, ORB), BF),
            vmem((OWN, 2 * ORB, 2 * ORB), BF),
            vmem((OWN, 2, 2 * ORB, ORB), BF),
            vmem((STEPS, ORB, BAND), F32),
            vmem((STEPS, ORB, BAND), F32),
            vmem((4, OWN - 1, ORB, BAND), F32),
            vmem((STEPS, ORB, BAND), F32),
            dma((7,)),
            dma((near,)),
            dma((near,)),
            dma((near,)),
            dma((near,)),
            dma((PLANES,)),
            dma((PLANES,)),
            dma((PER,)),
            dma((PLANES - 1, PER)),
            dma((SLABS,)),
            dma((SLABS, ROW - 1)),
            dma((SLABS, ROW)),
            dma((SLABS,)),
            dma((SLABS,)),
            dma((STEPS,)),
            dma((STEPS,)),
            dma((STEPS,)),
            dma((BLOCKS + PER,)),
        ],
        compiler_params=pltpu.CompilerParams(
            collective_id=0, has_side_effects=True, vmem_limit_bytes=60 << 20
        ),
    )(
        mode_shifts,
        occupancy,
        onsite,
        jnp.swapaxes(sigma_real, 0, 1),
        jnp.swapaxes(broadening, 0, 1),
        couplings,
        mode_weights,
    )
    shape = (PLANES, PER, ORB, BAND)
    return out[:SLABS].reshape(shape), out[SLABS:BLOCKS].reshape(shape)


def solution(mesh):
    in_specs = (
        P("chain", None),
        P("energy", "chain", None),
        P("energy", "chain", None),
        P("chain", None, None),
        P("energy", "chain"),
        P(),
        P(),
    )
    out_specs = (P("energy", "chain", None, None), P("energy", "chain", None, None))
    return jax.shard_map(body, mesh=mesh, in_specs=in_specs, out_specs=out_specs, check_vma=False)
```

```python
import jax
import jax.numpy as jnp
from jax import lax
from jax.experimental import pallas as pl
from jax.experimental.pallas import tpu as pltpu
from jax.sharding import PartitionSpec as P

ORB = 256
HALF = 128
BAND = 128
SHIFT = 24
SLABS = 12
PLANES = 4
PER = 3
ENERGIES = 256
NEAR = 3
OWN = 3
PICK = 4
STEPS = 2 * SLABS
ROW = 4
PIECE = HALF // ROW
BLOCKS = 2 * PLANES * PER
AHEAD = 1
GROUPS = ((0,), (1,)) + tuple((t, t + 1) for t in range(2, 22, 2)) + ((22,), (23,))
BF = jnp.bfloat16
F32 = jnp.float32
MESH = pl.DeviceIdType.MESH


def split(value):
    high = value.astype(BF)
    low = (value - high.astype(F32)).astype(BF)
    return high, low


def split3(value):
    high, rest = split(value)
    low = (value - high.astype(F32) - rest.astype(F32)).astype(BF)
    return high, rest, low


def dot(a, b):
    return jnp.dot(a, b, preferred_element_type=F32)


def dot_nt(a, b):
    return lax.dot_general(a, b, (((1,), (1,)), ((), ())), preferred_element_type=F32)


def sweep_kernel(
    shifts_in, filled_in, onsite_in, sigma_in, broadening_in, couplings_in, weights_in, out,
    shifts, filled, onsite, sigma_real, broadening, couplings, weights, cast,
    win, picked, props, cfull, cmat, ctmat, state, wide, sent, got, band, stage,
    in_s, win_s, win_r, join_s, join_r, pick_s, pick_r,
    c0_s, c1_s, c1_r, c2_s, c2_r, c3_s, c3_r, ex_s, ex_r, out_s, out_r,
):
    loads = [
        pltpu.make_async_copy(source, target, in_s.at[i])
        for i, (source, target) in enumerate(
            (
                (couplings_in, couplings),
                (onsite_in, onsite),
                (sigma_in, sigma_real),
                (broadening_in, broadening),
                (filled_in, filled),
                (weights_in, weights),
                (shifts_in, shifts),
            )
        )
    ]
    for load in loads:
        load.start()

    me_e = lax.axis_index("energy")
    me_y = lax.axis_index("chain")
    devices = lax.axis_size("energy")
    chips = devices // 2
    chip = me_e // 2
    core = lax.rem(me_e, 2)
    sign = 1 - 2 * core
    other = me_e + sign
    me_x = me_e // (devices // ROW)

    rows = lax.broadcasted_iota(jnp.int32, (ORB, ORB), 0)
    cols = lax.broadcasted_iota(jnp.int32, (ORB, ORB), 1)
    anti = rows + cols == ORB - 1
    flip = jnp.where(anti, 1.0, 0.0).astype(BF)
    flip8 = 7 - lax.broadcasted_iota(jnp.int32, (8, BAND), 0)

    def near(j):
        return lax.rem(chip + j + chips, chips) * 2 + core

    def beside(i):
        return lax.rem(me_e + i * (devices // ROW), devices)

    def plane(step):
        return lax.rem(me_y + step, PLANES)

    def remote(source, target, send_sem, recv_sem, e, y):
        return pltpu.make_async_remote_copy(
            src_ref=source,
            dst_ref=target,
            send_sem=send_sem,
            recv_sem=recv_sem,
            device_id=(e, y),
            device_id_type=MESH,
        )

    barrier = pltpu.get_barrier_semaphore()
    peers = [(near(j), me_y) for j in range(-NEAR, NEAR + 1) if j]
    peers += [(beside(i), me_y) for i in range(1, ROW)]
    peers += [(me_e, plane(step)) for step in range(1, PLANES)]
    peers += [(other, plane(step)) for step in range(PLANES)]
    for peer in peers:
        pl.semaphore_signal(barrier, inc=1, device_id=peer, device_id_type=MESH)

    mine = (2 * NEAR + core) * 4
    for load in loads[1:]:
        load.wait()
    points = (me_e * 4 + lax.broadcasted_iota(jnp.int32, (4, ORB), 0)).astype(F32)
    energy = -3.0 + 6.0 * (points + 0.5) / ENERGIES
    for sl in range(PER):
        detuning = energy - onsite[sl : sl + 1] - sigma_real[sl]
        width = broadening[sl]
        scale = detuning * detuning + width * width
        real = detuning / scale
        imag = -width / scale
        for i in range(4):
            for h in range(2):
                lanes = slice(HALF * h, HALF * (h + 1))
                win[mine + i, 4 * sl + h : 4 * sl + h + 1] = real[i : i + 1, lanes]
                win[mine + i, 4 * sl + 2 + h : 4 * sl + 3 + h] = imag[i : i + 1, lanes]
            win[mine + i, 12 + sl : 13 + sl] = jnp.broadcast_to(filled[i : i + 1, sl : sl + 1], (1, HALF))
    for i in range(4):
        win[mine + i, 15:16] = jnp.zeros((1, HALF), F32)

    loads[0].wait()
    for j in range(PER):
        cast[j] = couplings[j].astype(F32)

    pl.semaphore_wait(barrier, len(peers))

    def window(j):
        return remote(
            win.at[pl.ds(mine, 4)],
            win.at[pl.ds(((NEAR - j) * 2 + core) * 4, 4)],
            win_s.at[j + NEAR],
            win_r.at[NEAR - j],
            near(j),
            me_y,
        )

    def join(j):
        part = win.at[pl.ds(((NEAR + j) * 2 + core) * 4, 4)]
        return remote(part, part, join_s.at[j + NEAR], join_r.at[j + NEAR], other, me_y)

    def joined(j):
        part = win.at[pl.ds(((NEAR + j) * 2 + 1 - core) * 4, 4)]
        return remote(part, part, join_s.at[j + NEAR], join_r.at[j + NEAR], other, me_y)

    far_first = (3, -3, 2, -2, 1, -1)
    for j in far_first:
        window(j).start()
    join(0).start()

    piece = core * HALF + me_x * PIECE

    def part_of(s, x):
        return cfull.at[s, pl.ds(core * HALF + x * PIECE, PIECE)]

    def coupling_out(step, j):
        s = me_y * PER + j
        return remote(
            cast.at[j, pl.ds(piece, PIECE)],
            part_of(s, me_x),
            c1_s.at[step - 1, j],
            c1_r.at[s],
            me_e,
            plane(step),
        )

    def coupling_sends(j, act):
        for step in (1, 3, 2):
            act(coupling_out(step, j))

    @pl.when(me_y > 0)
    def _():
        coupling_sends(0, lambda c: c.start())

    coupling_sends(1, lambda c: c.start())
    coupling_sends(2, lambda c: c.start())

    def coupling_here(j, i):
        x = lax.rem(me_x + i, ROW)
        s = me_y * PER + j
        sem = c2_r.at[s, x] if i else c0_s.at[j]
        return pltpu.make_async_copy(
            cast.at[j, pl.ds(core * HALF + x * PIECE, PIECE)], part_of(s, x), sem
        )

    for j in range(PER):
        for i in range(ROW):
            coupling_here(j, i).start()

    def coupling_beside(s, i):
        part = part_of(s, me_x)
        return remote(part, part, c2_s.at[s, i - 1], c2_r.at[s, me_x], beside(i), me_y)

    def along_row(s):
        @pl.when(s // PER != me_y)
        def _():
            part = part_of(s, me_x)
            remote(part, part, c1_s.at[0, 0], c1_r.at[s], me_e, s // PER).wait_recv()
            for i in (1, 3, 2):
                coupling_beside(s, i).start()

    along_row(1)

    for j in far_first[::-1]:
        part = win.at[pl.ds(((NEAR + j) * 2 + core) * 4, 4)]
        remote(part, part, win_s.at[0], win_r.at[NEAR + j], other, me_y).wait_recv()
        join(j).start()
    for j in (0,) + far_first[::-1]:
        joined(j).wait_recv()

    s2 = shifts[2] * sign
    s3 = shifts[3] * sign
    offsets = (SHIFT * sign, s2, s3, -SHIFT * sign)
    for y in range(PLANES):
        for phase in range(2):
            for k in range(PICK):
                value = win[SHIFT + 4 * phase + y + offsets[k]]
                picked[y, :, phase * PICK + k, :] = value

    def pick_out(step):
        return remote(
            picked.at[plane(step)],
            props.at[me_y],
            pick_s.at[step],
            pick_r.at[me_y],
            me_e,
            plane(step),
        )

    pick_here = pltpu.make_async_copy(picked.at[me_y], props.at[me_y], pick_s.at[0])
    for step in (2, 1, 3):
        pick_out(step).start()
    pick_here.start()
    for s in range(2, SLABS):
        along_row(s)

    def pass_on(s):
        part = cfull.at[s, pl.ds(core * HALF, HALF)]
        return remote(part, part, c3_s.at[s], c3_r.at[s], other, me_y)

    def forward(s):
        for i in range(1, ROW):
            x = lax.rem(me_x + i, ROW)
            part = part_of(s, x)
            remote(part, part, c1_s.at[0, 0], c2_r.at[s, x], other, me_y).wait_recv()
        pass_on(s).start()

    def ready(s):
        part = cfull.at[s, pl.ds((1 - core) * HALF, HALF)]
        remote(part, part, c3_s.at[s], c3_r.at[s], other, me_y).wait_recv()

    for j in range(PER):
        coupling_here(j, 0).wait()
    for s in range(1, AHEAD + 1):
        forward(s)

    pick_here.wait()
    for step in range(1, PLANES):
        source = plane(step)
        remote(
            picked.at[0], props.at[source], pick_s.at[step], pick_r.at[source], me_e, source
        ).wait_recv()

    def keep(k, t, gr, gi):
        high, low = split(gr)
        state[k, 0:ORB, 0:ORB] = high
        state[k, 0:ORB, ORB:] = low
        high, low = split(gi)
        state[k, ORB:, 0:ORB] = high
        state[k, ORB:, ORB:] = low
        rolled = pltpu.roll(gi, 1, 1, stride=1, stride_axis=0)[:, :BAND]
        if k == 0:
            sent[t] = rolled
        else:
            band[t % 4, k - 1] = rolled

    def exchange(t):
        return remote(sent.at[t], got.at[t], ex_s.at[t], ex_r.at[t], other, me_y)

    def ship(t):
        phase, s = t // SLABS, t % SLABS
        p, sl = s // PER, s % PER
        here = 1 - (lax.rem(p - me_y + PLANES, PLANES) + PLANES - 1) // PLANES
        here = here * (core if phase else 1 - core)
        base = (core * PLANES + me_y) * PER + sl
        at = base + here * (BLOCKS + sl - base)
        owner = chip * 2 + phase
        return remote(
            stage.at[t], out.at[at], out_s.at[t], out_r.at[at], owner + here * sign, p
        )

    def ship_here(sl):
        at = (core * PLANES + me_y) * PER + sl
        return pltpu.make_async_copy(
            stage.at[core * SLABS + me_y * PER + sl], out.at[at], c0_s.at[sl]
        )

    def factors(phase):
        first = chip * 8 + 4 * phase + me_y
        result = []
        for k, m in enumerate((0, 2, 3, 1)):
            e = first + offsets[k]
            scale = jnp.where((e >= 0) & (e < ENERGIES), -2.0, 0.0)
            result.append(scale * weights[m : m + 1, :])
        return result

    core_f = core.astype(F32)
    sign_f = sign.astype(F32)

    def finish(t, phase):
        s = t % SLABS
        fill = props[s // PER, 12 + s % PER]
        w = []
        for k, factor in enumerate(factors(phase)):
            w.append(factor * (core_f + sign_f * fill[phase * PICK + k : phase * PICK + k + 1]))
        slot = t % 4
        for i in range(ORB // 8):
            at = slice(8 * i, 8 * i + 8)
            x = sent[t, at] * w[0] + band[slot, 0, at] * w[1]
            x += band[slot, 1, at] * w[2] + got[t, at] * w[3]
            x = jnp.take_along_axis(x, flip8, axis=0)
            u = ORB // 8 - 1 - i
            stage[t, 8 * u : 8 * u + 8] = x

    def prop_rows(s, phase):
        p, sl = s // PER, s % PER
        at = slice(phase * PICK, phase * PICK + OWN)
        tiles = [props[p, 4 * sl + q][at] for q in range(4)]
        return jnp.concatenate(tiles[:2], axis=1), jnp.concatenate(tiles[2:], axis=1)

    def start(phase):
        real, imag = prop_rows(0, phase)
        for k in range(OWN):
            keep(
                k,
                phase * SLABS,
                jnp.where(anti, real[k : k + 1], 0.0),
                jnp.where(anti, imag[k : k + 1], 0.0),
            )

    def slab(s, phase):
        t = phase * SLABS + s
        if phase == 0:
            c = cfull[s].astype(BF)
            ct = dot(dot_nt(flip, c).astype(BF), flip).astype(BF)
            cmat[s] = c
            ctmat[s] = ct
        c2 = jnp.concatenate([cmat[s], cmat[s]], axis=0)
        ct2 = jnp.concatenate([ctmat[s], ctmat[s]], axis=1)
        real, imag = prop_rows(s, phase)
        both = jnp.concatenate([real, imag, jnp.zeros((2, ORB), F32)], axis=0)
        columns = dot_nt(
            jnp.concatenate([flip, flip, flip], axis=1),
            jnp.concatenate(split3(both), axis=1),
        )

        def first(k):
            inner = dot(state[k], c2)
            high, low = split(inner)
            wide[k, 0, 0:ORB] = high[:ORB]
            wide[k, 0, ORB:] = low[:ORB]
            wide[k, 1, 0:ORB] = high[ORB:]
            wide[k, 1, ORB:] = low[ORB:]

        def second(k):
            hr = dot(ct2, wide[k, 0])
            hi = dot(ct2, wide[k, 1])
            rr = real[k : k + 1]
            ri = imag[k : k + 1]
            cr = columns[:, k : k + 1]
            ci = columns[:, OWN + k : OWN + k + 1]
            qr = hr * rr - hi * ri
            qi = hr * ri + hi * rr
            qr = jnp.where(anti, qr + 1.0, qr)
            keep(k, t, qr * cr - qi * ci, qr * ci + qi * cr)

        for k in range(OWN):
            first(k)
        for k in range(OWN):
            second(k)

    def conclude(group):
        for t in group:
            exchange(t).wait_recv()
        for t in group:
            finish(t, t // SLABS)
            ship(t).start()

    for i, group in enumerate(GROUPS):
        for t in group:
            if t % SLABS:
                slab(t % SLABS, t // SLABS)
            else:
                start(t // SLABS)
        for t in group:
            exchange(t).start()
        after = GROUPS[i + 1] if i + 1 < len(GROUPS) else ()
        for t in after:
            if t < SLABS:
                ready(t)
        for t in GROUPS[i + 2] if i + 2 < len(GROUPS) else ():
            if AHEAD < t < SLABS:
                forward(t)
        if i:
            conclude(GROUPS[i - 1])
    conclude(GROUPS[-1])

    for sl in range(PER):
        ship_here(sl).start()

    for j in far_first:
        window(j).wait_send()
    for j in range(-NEAR, NEAR + 1):
        join(j).wait_send()
    for step in range(1, PLANES):
        pick_out(step).wait_send()

    @pl.when(me_y > 0)
    def _():
        coupling_sends(0, lambda c: c.wait_send())

    coupling_sends(1, lambda c: c.wait_send())
    coupling_sends(2, lambda c: c.wait_send())
    for i in range(1, ROW):
        @pl.when(me_y == 0)
        def _(i=i):
            coupling_here(0, i).wait()

    def passed(s, _):
        pass_on(s).wait_send()

        @pl.when(s // PER != me_y)
        def _():
            for i in range(1, ROW):
                coupling_beside(s, i).wait_send()

        return 0

    lax.fori_loop(1, SLABS, passed, 0)

    def shipped(t, _):
        exchange(t).wait_send()
        remote(stage.at[t], out.at[0], out_s.at[t], out_r.at[0], other, me_y).wait_send()
        return 0

    lax.fori_loop(0, STEPS, shipped, 0)

    def landed(i, _):
        @pl.when(i // PER != core * PLANES + me_y)
        def _():
            remote(stage.at[0], out.at[i], out_s.at[0], out_r.at[i], other, me_y).wait_recv()

        return 0

    lax.fori_loop(0, BLOCKS + PER, landed, 0)
    for sl in range(PER):
        ship_here(sl).wait()


def body(onsite, sigma_real, broadening, couplings, occupancy, mode_weights, mode_shifts):
    hbm = pl.BlockSpec(memory_space=pltpu.HBM)
    vmem = pltpu.VMEM
    dma = pltpu.SemaphoreType.DMA
    near = 2 * NEAR + 1
    out = pl.pallas_call(
        sweep_kernel,
        out_shape=jax.ShapeDtypeStruct((BLOCKS + PER, ORB, BAND), F32),
        in_specs=[hbm] * 7,
        out_specs=pl.BlockSpec(memory_space=pl.ANY),
        scratch_shapes=[
            pltpu.SMEM(mode_shifts.shape, jnp.int32),
            vmem(occupancy.shape, F32),
            vmem(onsite.shape, F32),
            vmem((PER, 4, ORB), F32),
            vmem((PER, 4, ORB), F32),
            vmem(couplings.shape, BF),
            vmem(mode_weights.shape, F32),
            vmem((PER, ORB, ORB), F32),
            vmem((8 * near, 16, HALF), F32),
            vmem((PLANES, 16, 8, HALF), F32),
            vmem((PLANES, 16, 8, HALF), F32),
            vmem((SLABS, ORB, ORB), F32),
            vmem((SLABS, ORB, ORB), BF),
            vmem((SLABS, ORB, ORB), BF),
            vmem((OWN, 2 * ORB, 2 * ORB), BF),
            vmem((OWN, 2, 2 * ORB, ORB), BF),
            vmem((STEPS, ORB, BAND), F32),
            vmem((STEPS, ORB, BAND), F32),
            vmem((4, OWN - 1, ORB, BAND), F32),
            vmem((STEPS, ORB, BAND), F32),
            dma((7,)),
            dma((near,)),
            dma((near,)),
            dma((near,)),
            dma((near,)),
            dma((PLANES,)),
            dma((PLANES,)),
            dma((PER,)),
            dma((PLANES - 1, PER)),
            dma((SLABS,)),
            dma((SLABS, ROW - 1)),
            dma((SLABS, ROW)),
            dma((SLABS,)),
            dma((SLABS,)),
            dma((STEPS,)),
            dma((STEPS,)),
            dma((STEPS,)),
            dma((BLOCKS + PER,)),
        ],
        compiler_params=pltpu.CompilerParams(
            collective_id=0, has_side_effects=True, vmem_limit_bytes=60 << 20
        ),
    )(
        mode_shifts,
        occupancy,
        onsite,
        jnp.swapaxes(sigma_real, 0, 1),
        jnp.swapaxes(broadening, 0, 1),
        couplings,
        mode_weights,
    )
    shape = (PLANES, PER, ORB, BAND)
    return out[:SLABS].reshape(shape), out[SLABS:BLOCKS].reshape(shape)


def solution(mesh):
    in_specs = (
        P("chain", None),
        P("energy", "chain", None),
        P("energy", "chain", None),
        P("chain", None, None),
        P("energy", "chain"),
        P(),
        P(),
    )
    out_specs = (P("energy", "chain", None, None), P("energy", "chain", None, None))
    return jax.shard_map(body, mesh=mesh, in_specs=in_specs, out_specs=out_specs, check_vma=False)
```
